32 devices in a mesh: replica: 16 (over z, y, x), tensor: 2 (over core).
Axes of the slice: x: 2, y: 2, z: 4, core: 2. Of those that a mesh axis runs over, the one named last changes fastest.
Arguments:
- lengths: int32 [256], replicated, may hold values from 1 to 254, as said below
- page_table: int32 [256, 2], P('replica'), may hold values from 0 to 31, as said below
- key_pool: bfloat16 [512, 128, 1024], P('replica', None, 'tensor'), may hold values from -4 to 4
- value_pool: bfloat16 [512, 128, 1024], P('replica', None, 'tensor'), may hold values from -5 to 5
- queries: bfloat16 [2, 256, 4096], P(None, 'replica', 'tensor'), may hold values from -80 to 80
- new_keys: bfloat16 [2, 256, 1024], P(None, 'replica', 'tensor'), may hold values from -4 to 4
- new_values: bfloat16 [2, 256, 1024], P(None, 'replica', 'tensor'), may hold values from -5 to 5
- conv_state: float32 [256, 3, 8192], P('replica', None, 'tensor'), may hold values from -5 to 5
- ssm_state: float32 [256, 16, 8192], P('replica', None, 'tensor'), may hold values from -5 to 5
- mamba_x: bfloat16 [2, 256, 8192], P(None, 'replica', 'tensor'), may hold values from -5 to 5
- mamba_z: bfloat16 [2, 256, 8192], P(None, 'replica', 'tensor'), may hold values from -5 to 5
- conv_weight: float32 [4, 8192], P(None, 'tensor'), may hold values from -3 to 3
- conv_bias: float32 [8192], P('tensor'), may hold values from -3 to 3
- dt_down: bfloat16 [8192, 256], P('tensor'), may hold values from -0.0625 to 0.0625
- bc_proj: bfloat16 [8192, 32], P('tensor'), may hold values from -0.0625 to 0.0625
- dt_up: bfloat16 [256, 8192], P(None, 'tensor'), may hold values from -0.375 to 0.375
- dt_bias: float32 [8192], P('tensor'), may hold values from -3 to 0
- a_log: float32 [16, 8192], P(None, 'tensor'), may hold values from 0 to 2.77
- skip_d: float32 [8192], P('tensor'), may hold values from 0.5 to 2
- moves: int32 [128, 2], replicated, may hold values from 0 to 255, as said below
Outputs:
- attention: bfloat16 [2, 256, 4096], P(None, 'replica', 'tensor')
- mamba_out: bfloat16 [2, 256, 8192], P(None, 'replica', 'tensor')
- final_ssm: float32 [256, 16, 8192], P('replica', None, 'tensor')
- final_conv: float32 [256, 3, 8192], P('replica', None, 'tensor')
The draws below stay inside these ranges and needn't reach their ends.
Inputs may be any that keep to these rules, and one draw needn't show every extreme that they name: `lengths`: each replica has one request of the longest length. `page_table`: the rows of the 16 requests of one replica name each of that replica's 32 pages once. `moves`: rows r * 8 to r * 8 + 7 are the 8 requests that leave replica r, each to another replica, no two to the same one; every replica receives 8 requests, from 8 different replicas, into exactly the slots that its own leaving requests free; the j-th row of every replica goes the same number of replicas further along, counted modulo the number of replicas; one of these numbers is 1 and another is half the number of replicas.
All inputs are finite; a program needn't handle non-finite values.
Results may differ from the reference program's by a relative error of at most 0.013.
Values may be sent and summed in bfloat16 or wider, within the bound.
A program may use at most 128 MiB of HBM per device.

```python
import math
import jax
import jax.numpy as jnp
from jax import lax

HQ = 32
KVH = 8
HD = 128
INNER = 8192
DS = 16
DT_RANK = 256
CONV = 4
PAGE = 128
MAXP = 2
SLOTS = 16
MOVES = 8
REQ = 256
POOL = 32
NPAGES = 512
CTX = 256
N_REPLICA = 16


def length_table(key):
    key = jax.random.fold_in(key, 201)
    replica_scale = jax.random.randint(jax.random.fold_in(key, 1), (N_REPLICA, 1), 1, 5)
    drawn_len = jax.random.randint(jax.random.fold_in(key, 2), (N_REPLICA, SLOTS), 0, CTX - 2)
    lengths_all = (1 + drawn_len * replica_scale // 4).reshape(REQ)
    chosen = jax.random.randint(jax.random.fold_in(key, 3), (N_REPLICA,), 0, SLOTS) + jnp.arange(N_REPLICA) * SLOTS
    longest = jnp.any(jnp.arange(REQ)[:, None] == chosen[None, :], axis=1)
    return jnp.where(longest, CTX - 2, lengths_all).astype(jnp.int32)


def page_layout(key):
    keys_all = jax.random.split(jax.random.fold_in(key, 202), N_REPLICA)
    orders = jax.vmap(lambda sub_key: jax.random.permutation(sub_key, POOL))(keys_all)
    return orders.reshape(REQ, MAXP).astype(jnp.int32)


def move_plan(key):
    key = jax.random.fold_in(key, 203)
    candidates = jnp.arange(1, N_REPLICA, dtype=jnp.int32)
    priority = jax.random.permutation(jax.random.fold_in(key, 1), N_REPLICA - 1).astype(jnp.int32)
    priority = jnp.where(candidates == 1, -2, jnp.where(candidates == N_REPLICA // 2, -1, priority))
    order = jnp.argsort(priority, stable=True)
    offsets = candidates[order][:MOVES]
    keys_all = jax.random.split(jax.random.fold_in(key, 2), N_REPLICA)
    leaving = jax.vmap(lambda sub_key: jax.random.permutation(sub_key, SLOTS)[:MOVES])(keys_all)
    replica_ids = jnp.arange(N_REPLICA)[:, None]
    target = (replica_ids + offsets[None, :]) % N_REPLICA
    columns = jnp.arange(MOVES)[None, :]
    source_slot = replica_ids * SLOTS + leaving
    target_slot = target * SLOTS + leaving[target, columns]
    return jnp.stack([source_slot.reshape(-1), target_slot.reshape(-1)], axis=1).astype(jnp.int32)


def fresh_keys(key):
    return jax.random.truncated_normal(jax.random.fold_in(key, 204), -4.0, 4.0, (2, REQ, KVH * HD), jnp.float32)


def draw_lengths(key, part):
    return length_table(key)


def draw_page_table(key, part):
    return page_layout(key)


def draw_moves(key, part):
    return move_plan(key)


def draw_new_keys(key, part):
    return fresh_keys(key).astype(jnp.bfloat16)


def draw_queries(key, part):
    key = jax.random.fold_in(key, 3)
    drawn = 2.0 * jax.random.truncated_normal(key, -4.0, 4.0, (2, REQ, HQ * HD), jnp.float32)
    return drawn.astype(jnp.bfloat16)


def draw_key_pool(key, part):
    key = jax.random.fold_in(key, 5)
    pool = jax.random.truncated_normal(key, -4.0, 4.0, (NPAGES, PAGE, KVH * HD), jnp.float32)
    return pool.astype(jnp.bfloat16)


def level_of(own_key, shape, shards, least, high):
    level = 1.0
    for dim, parts in shards:
        heights = jax.random.uniform(jax.random.fold_in(jax.random.fold_in(own_key, 6), dim), (parts,), jnp.float32, least / len(shards), high / len(shards))
        level = level * jnp.repeat(jnp.exp(heights), shape[dim] // parts).reshape((-1,) + (1,) * (len(shape) - 1 - dim))
    return level


def scatter_about(key, dims, width, most, cuts=(), held_as=jnp.bfloat16):
    values = width * jax.random.normal(key, dims, jnp.float32)
    if cuts:
        values = values * level_of(key, dims, cuts, -0.22, 0.18)
    return jnp.clip(values, -most, most).astype(held_as)


def setup_inputs(seed: int = 0) -> dict:
    arg_keys = jax.random.split(jax.random.key(seed), 21)
    lengths = draw_lengths(jax.random.fold_in(arg_keys[20], 71), 0)
    page_table = draw_page_table(jax.random.fold_in(arg_keys[20], 71), 0)
    key_pool = draw_key_pool(jax.random.fold_in(arg_keys[20], 71), 0)
    value_pool = scatter_about(arg_keys[3], (NPAGES, PAGE, KVH * HD), 1.0, 5.0, ((0, 16), (2, 2)))
    queries = draw_queries(jax.random.fold_in(arg_keys[20], 71), 0)
    new_keys = draw_new_keys(jax.random.fold_in(arg_keys[20], 71), 0)
    new_values = scatter_about(arg_keys[6], (2, REQ, KVH * HD), 1.0, 5.0, ((1, 16), (2, 2)))
    conv_state = scatter_about(arg_keys[7], (REQ, CONV - 1, INNER), 1.0, 5.0, ((0, 16), (2, 2)), jnp.float32)
    ssm_state = scatter_about(arg_keys[8], (REQ, DS, INNER), 1.0, 5.0, ((0, 16), (2, 2)), jnp.float32)
    mamba_x = scatter_about(arg_keys[9], (2, REQ, INNER), 1.0, 5.0, ((1, 16), (2, 2)))
    mamba_z = scatter_about(arg_keys[10], (2, REQ, INNER), 1.0, 5.0, ((1, 16), (2, 2)))
    conv_weight = scatter_about(arg_keys[11], (CONV, INNER), CONV ** -0.5, 3.0, ((1, 2),), jnp.float32)
    conv_bias = scatter_about(arg_keys[12], (INNER,), 0.5, 3.0, ((0, 2),), jnp.float32)
    dt_down = scatter_about(arg_keys[13], (INNER, DT_RANK), INNER ** -0.5, 0.0625, ((0, 2),))
    bc_proj = scatter_about(arg_keys[14], (INNER, 2 * DS), INNER ** -0.5, 0.0625, ((0, 2),))
    dt_up = scatter_about(arg_keys[15], (DT_RANK, INNER), DT_RANK ** -0.5, 0.375, ((1, 2),))
    dt_bias = jnp.clip(-3.0 + 3.0 * jax.random.uniform(arg_keys[16], (INNER,), jnp.float32) ** level_of(arg_keys[16], (INNER,), ((0, 2),), -0.2, 0.2), -3.0, 0.0)
    a_log = jnp.clip(2.77 * jax.random.uniform(arg_keys[17], (DS, INNER), jnp.float32) ** level_of(arg_keys[17], (DS, INNER), ((1, 2),), -0.2, 0.2), 0.0, 2.77)
    skip_d = jnp.clip(0.5 + 1.5 * jax.random.uniform(arg_keys[18], (INNER,), jnp.float32) ** level_of(arg_keys[18], (INNER,), ((0, 2),), -0.2, 0.2), 0.5, 2.0)
    moves = draw_moves(jax.random.fold_in(arg_keys[20], 71), 0)
    return dict(lengths=lengths, page_table=page_table, key_pool=key_pool, value_pool=value_pool, queries=queries, new_keys=new_keys, new_values=new_values, conv_state=conv_state, ssm_state=ssm_state, mamba_x=mamba_x, mamba_z=mamba_z, conv_weight=conv_weight, conv_bias=conv_bias, dt_down=dt_down, bc_proj=bc_proj, dt_up=dt_up, dt_bias=dt_bias, a_log=a_log, skip_d=skip_d, moves=moves)


def attend(query_rows, key_rows, value_rows, last_pos):
    rows_count = query_rows.shape[0]
    key_span = key_rows.shape[1]
    kv_heads = key_rows.shape[2] // HD
    group_size = query_rows.shape[1] // key_rows.shape[2]
    query_heads = query_rows.reshape(rows_count, kv_heads, group_size, HD).astype(jnp.float32)
    key_heads = key_rows.reshape(rows_count, key_span, kv_heads, HD).astype(jnp.float32)
    value_heads = value_rows.reshape(rows_count, key_span, kv_heads, HD).astype(jnp.float32)
    scores = jnp.einsum('skgd,spkd->skgp', query_heads, key_heads) * (1.0 / math.sqrt(HD))
    visible = jnp.arange(key_span)[None, :] <= last_pos[:, None]
    scores = jnp.where(visible[:, None, None, :], scores, -1e+30)
    largest = lax.optimization_barrier(jnp.max(scores, axis=-1, keepdims=True))
    exponent = jnp.exp(scores - largest)
    weights = (exponent / lax.optimization_barrier(jnp.sum(exponent, axis=-1, keepdims=True))).astype(jnp.bfloat16)
    attended = jnp.einsum('skgp,spkd->skgd', weights.astype(jnp.float32), value_heads)
    return attended.astype(jnp.bfloat16).reshape(rows_count, query_rows.shape[1])

def attend_all(query_rows, key_rows, value_rows, last_pos):
    grouped = (query_rows.reshape(N_REPLICA, SLOTS, query_rows.shape[1]), key_rows.reshape(N_REPLICA, SLOTS, CTX, key_rows.shape[2]), value_rows.reshape(N_REPLICA, SLOTS, CTX, value_rows.shape[2]), last_pos.reshape(N_REPLICA, SLOTS))
    result = lax.map(lambda pieces: attend(pieces[0], pieces[1], pieces[2], pieces[3]), grouped)
    return result.reshape(REQ, query_rows.shape[1])

def mamba_step(conv_prev, state_prev, x_in, z_in, params):
    conv_weight, conv_bias, dt_down, bc_proj, dt_up, dt_bias, a_log, skip_d = params
    window = jnp.concatenate([conv_prev, x_in.astype(jnp.float32)[:, None, :]], axis=1)
    conv_out = jax.nn.silu(lax.optimization_barrier(jnp.sum(window * conv_weight[None], axis=1)) + conv_bias)
    mixed_in = conv_out.astype(jnp.bfloat16)
    low_rank = jnp.dot(mixed_in, dt_down, preferred_element_type=jnp.float32)
    bc_terms = jnp.dot(mixed_in, bc_proj, preferred_element_type=jnp.float32)
    dt_step = jax.nn.softplus(jnp.dot(low_rank.astype(jnp.bfloat16), dt_up, preferred_element_type=jnp.float32) + dt_bias)
    state_count = a_log.shape[0]
    b_in = bc_terms[:, :state_count]
    c_out = bc_terms[:, state_count:]
    inputs_wide = mixed_in.astype(jnp.float32)
    decay_rate = jnp.exp(-dt_step[:, None, :] * jnp.exp(a_log)[None])
    state_new = decay_rate * state_prev + dt_step[:, None, :] * b_in[:, :, None] * inputs_wide[:, None, :]
    output = (lax.optimization_barrier(jnp.sum(c_out[:, :, None] * state_new, axis=1)) + skip_d * inputs_wide) * jax.nn.silu(z_in.astype(jnp.float32))
    return (output.astype(jnp.bfloat16), window[:, 1:], state_new)

def reference(lengths, page_table, key_pool, value_pool, queries, new_keys, new_values, conv_state, ssm_state, mamba_x, mamba_z, conv_weight, conv_bias, dt_down, bc_proj, dt_up, dt_bias, a_log, skip_d, moves):
    params = (conv_weight, conv_bias, dt_down, bc_proj, dt_up, dt_bias, a_log, skip_d)
    request_ids = jnp.arange(REQ, dtype=jnp.int32)
    page_rows = (request_ids // SLOTS * POOL)[:, None] + page_table
    key_cache = key_pool[page_rows].reshape(REQ, CTX, KVH * HD).at[request_ids, lengths].set(new_keys[0])
    value_cache = value_pool[page_rows].reshape(REQ, CTX, KVH * HD).at[request_ids, lengths].set(new_values[0])
    attention_one = attend_all(queries[0], key_cache, value_cache, lengths)
    mamba_one, conv_one, state_one = mamba_step(conv_state, ssm_state, mamba_x[0], mamba_z[0], params)
    source_slot = request_ids.at[moves[:, 1]].set(moves[:, 0].astype(jnp.int32))
    later_lengths = lengths[source_slot]
    later_keys = key_cache[source_slot].at[request_ids, later_lengths + 1].set(new_keys[1])
    later_values = value_cache[source_slot].at[request_ids, later_lengths + 1].set(new_values[1])
    attention_two = attend_all(queries[1], later_keys, later_values, later_lengths + 1)
    mamba_two, final_conv, final_ssm = mamba_step(conv_one[source_slot], state_one[source_slot], mamba_x[1], mamba_z[1], params)
    return (jnp.stack([attention_one, attention_two]), jnp.stack([mamba_one, mamba_two]), final_ssm, final_conv)
```

```python
import math

import jax
import jax.numpy as jnp
from jax import lax
from jax.sharding import PartitionSpec as P

HD = 128


def shards(
    lengths,
    page_table,
    key_pool,
    value_pool,
    queries,
    new_keys,
    new_values,
    conv_state,
    ssm_state,
    mamba_x,
    mamba_z,
    conv_weight,
    conv_bias,
    dt_down,
    bc_proj,
    dt_up,
    dt_bias,
    a_log,
    skip_d,
    moves,
):
    f32, bf16 = jnp.float32, jnp.bfloat16
    replica = lax.axis_index("replica")
    replicas = lax.axis_size("replica")
    slots = page_table.shape[0]
    span = page_table.shape[1] * key_pool.shape[1]
    width = key_pool.shape[2]
    kv_heads = width // HD
    group = queries.shape[2] // width
    channels = ssm_state.shape[2]
    states = ssm_state.shape[1]
    taps = conv_weight.shape[0]
    leaving = moves.shape[0] // replicas

    base = replica * slots
    mine = lax.dynamic_slice_in_dim(moves, replica * leaving, leaving, 0)
    leave_slot = mine[:, 0] - base
    shift = lax.rem(mine[:, 1] // slots - replica + replicas, replicas)
    from_rep = lax.rem(replica - shift + replicas, replicas)
    to_rep = mine[:, 1] // slots
    come = moves[from_rep * leaving + jnp.arange(leaving)]
    come_slot = come[:, 1] - base
    own_lengths = lax.dynamic_slice_in_dim(lengths, base, slots)
    lane_row = jnp.argmax(shift[None, :] == jnp.arange(1, replicas)[:, None], axis=1)

    scan_small = jnp.concatenate(
        [conv_state[leave_slot].astype(bf16), mamba_x[0][leave_slot][:, None]], axis=1
    ).reshape(leaving, taps * channels)
    asks = jnp.concatenate([queries[1], new_keys[1], new_values[1]], axis=1)
    forward = jnp.zeros((replicas, taps * channels), bf16).at[to_rep].set(scan_small)
    backward = jnp.zeros((replicas, asks.shape[1]), bf16).at[from_rep].set(asks[come_slot])
    small = lax.all_to_all(
        jnp.concatenate([forward, backward], axis=1),
        "replica",
        split_axis=0,
        concat_axis=0,
        tiled=True,
    )
    got_scan = small[from_rep, : taps * channels].reshape(leaving, taps, channels)
    got_asks = small[to_rep, taps * channels :]

    states16 = ssm_state.astype(bf16)
    lanes = []
    for k in range(1, replicas):
        block = states16[leave_slot[lane_row[k - 1]]]
        lanes.append(
            lax.ppermute(block, "replica", [(i, (i + k) % replicas) for i in range(replicas)])
        )

    asks_here = asks.at[leave_slot].set(got_asks)
    q2 = asks_here[:, : queries.shape[2]]
    k2 = asks_here[:, queries.shape[2] : queries.shape[2] + width]
    v2 = asks_here[:, queries.shape[2] + width :]
    slot_ids = jnp.arange(slots)
    heads = lambda t: t.reshape(t.shape[:-1] + (kv_heads, HD))
    keys = key_pool[page_table].reshape(slots, span, width)
    keys = keys.at[slot_ids, own_lengths].set(new_keys[0]).at[slot_ids, own_lengths + 1].set(k2)
    vals = value_pool[page_table].reshape(slots, span, width)
    vals = vals.at[slot_ids, own_lengths].set(new_values[0]).at[slot_ids, own_lengths + 1].set(v2)
    q = jnp.stack([queries[0], q2], axis=1).reshape(slots, 2, kv_heads, group, HD)
    scores = jnp.einsum("stkgd,spkd->sktgp", q, heads(keys), preferred_element_type=f32) * (
        1.0 / math.sqrt(HD)
    )
    last = own_lengths[:, None] + jnp.arange(2)[None]
    seen = jnp.arange(span)[None, None] <= last[:, :, None]
    scores = jnp.where(seen[:, None, :, None, :], scores, -1e30)
    expo = jnp.exp(scores - jnp.max(scores, axis=-1, keepdims=True))
    w = (expo / jnp.sum(expo, axis=-1, keepdims=True)).astype(bf16)
    att = jnp.einsum("sktgp,spkd->stkgd", w, heads(vals), preferred_element_type=f32)
    att = att.astype(bf16).reshape(slots, 2, queries.shape[2])
    back = jnp.zeros((replicas, queries.shape[2]), bf16).at[to_rep].set(att[leave_slot, 1])
    back = lax.all_to_all(back, "replica", split_axis=0, concat_axis=0, tiled=True)
    att_two = att[:, 1].at[come_slot].set(back[from_rep])

    proj = jnp.concatenate([dt_down, bc_proj], axis=1)
    rank = dt_down.shape[1]
    rate = jnp.exp(a_log)

    def front(win):
        xc = jax.nn.silu(jnp.sum(win * conv_weight[None], axis=1) + conv_bias).astype(bf16)
        both = lax.psum(jnp.dot(xc, proj, preferred_element_type=f32), "tensor")
        dt = jax.nn.softplus(
            jnp.dot(both[:, :rank].astype(bf16), dt_up, preferred_element_type=f32) + dt_bias
        )
        return xc.astype(f32), dt, both[:, rank : rank + states], both[:, rank + states :]

    def advance(h, xc, dt, b):
        return (
            jnp.exp(-dt[:, None, :] * rate[None]) * h
            + b[:, :, None] * (dt * xc)[:, None, :]
        )

    def emit(h, xc, c, z):
        out = jnp.sum(c[:, :, None] * h, axis=1) + skip_d * xc
        return (out * jax.nn.silu(z.astype(f32))).astype(bf16)

    win = jnp.concatenate([conv_state, mamba_x[0].astype(f32)[:, None]], axis=1)
    win = jnp.concatenate([win, got_scan.astype(f32)], axis=0)
    xc, dt, b, c = front(win)
    h_one = advance(ssm_state, xc[:slots], dt[:slots], b[:slots])
    mamba_one = emit(h_one, xc[:slots], c[:slots], mamba_z[0])

    win_two = win[:slots, 1:].at[come_slot].set(win[slots:, 1:])
    win_two = jnp.concatenate([win_two, mamba_x[1].astype(f32)[:, None]], axis=1)
    xc2, dt2, b2, c2 = front(win_two)

    got = jnp.stack(lanes)[shift - 1].astype(f32)
    h_got = advance(got, xc[slots:], dt[slots:], b[slots:])
    h_prev = h_one.at[come_slot].set(h_got)
    final_ssm = advance(h_prev, xc2, dt2, b2)
    mamba_two = emit(final_ssm, xc2, c2, mamba_z[1])
    return (
        jnp.stack([att[:, 0], att_two]),
        jnp.stack([mamba_one, mamba_two]),
        final_ssm,
        win_two[:, 1:],
    )


def solution(mesh):
    row, both = P("replica", None, "tensor"), P(None, "replica", "tensor")
    in_specs = (
        P(),
        P("replica", None),
        row,
        row,
        both,
        both,
        both,
        row,
        row,
        both,
        both,
        P(None, "tensor"),
        P("tensor"),
        P("tensor", None),
        P("tensor", None),
        P(None, "tensor"),
        P("tensor"),
        P(None, "tensor"),
        P("tensor"),
        P(),
    )
    return jax.shard_map(
        shards, mesh=mesh, in_specs=in_specs, out_specs=(both, both, row, row), check_vma=False
    )
```

```python
import functools
import math

import jax
import jax.numpy as jnp
from jax import lax
from jax.experimental import pallas as pl
from jax.experimental.pallas import tpu as pltpu
from jax.sharding import PartitionSpec as P

HD = 128
F32, BF16 = jnp.float32, jnp.bfloat16
MESH = pl.DeviceIdType.MESH
ANY = pl.BlockSpec(memory_space=pl.ANY)
VMEM = pl.BlockSpec(memory_space=pltpu.VMEM)
SMEM = pl.BlockSpec(memory_space=pltpu.SMEM)


def round_up(n, m):
    return (n + m - 1) // m * m


def silu(v):
    return v / (1.0 + jnp.exp(-v))


def softplus(v):
    return jnp.maximum(v, 0.0) + jnp.log1p(jnp.exp(-jnp.abs(v)))


def chunks(total):
    step = min(512, total)
    return [slice(i, i + step) for i in range(0, total, step)]


def exchange_kernel(
    sizes,
    moves,
    lengths,
    pages,
    keys_hbm,
    vals_hbm,
    asks,
    small,
    states_hbm,
    conv,
    mx,
    mz,
    conv_w,
    conv_b,
    down_hbm,
    bc_hbm,
    up_hbm,
    dt_b,
    a_log,
    skip,
    state_one,
    got_state,
    att,
    fconv,
    m_one,
    dt_moved,
    xc_moved,
    b_moved,
    dt_two,
    xc_two,
    b_two,
    c_two,
    table,
    keys,
    vals,
    h,
    down,
    bc_w,
    up,
    send_state,
    send_small,
    got_small,
    send_ask,
    got_ask,
    att_two,
    send_att,
    got_att,
    win,
    win_two,
    xc_all,
    dt_all,
    b_all,
    c_all,
    y,
    part,
    part_two,
    load_sem,
    state_s,
    state_r,
    small_s,
    small_r,
    ask_s,
    ask_r,
    att_s,
    att_r,
    part_s,
    part_r,
):
    R, T, S, L, H, KV = sizes
    C = small.shape[2] * 4
    N = a_log.shape[0]
    NR = win.shape[1]
    rank = down.shape[1]
    page = keys.shape[1]
    n_pages = pages.shape[1]
    me = lax.axis_index("replica")
    core = lax.axis_index("tensor")

    loads = [
        pltpu.make_async_copy(src, dst, load_sem.at[i])
        for i, (src, dst) in enumerate(
            [
                (states_hbm, h),
                (keys_hbm, keys),
                (vals_hbm, vals),
                (down_hbm, down),
                (bc_hbm, bc_w),
                (up_hbm, up),
            ]
        )
    ]
    for load in loads:
        load.start()

    barrier = pltpu.get_barrier_semaphore()

    def greet(k, _):
        pl.semaphore_signal(
            barrier, inc=1, device_id={"replica": lax.rem(me + k, R)}, device_id_type=MESH
        )
        return 0

    def greet_core(k, _):
        pl.semaphore_signal(
            barrier, inc=1, device_id={"tensor": lax.rem(core + k, T)}, device_id_type=MESH
        )
        return 0

    lax.fori_loop(1, R, greet, 0)
    lax.fori_loop(1, T, greet_core, 0)

    shift = [lax.div(moves[j, 1], S) for j in range(L)]
    out_slot = [lax.rem(moves[me * L + j, 0], S) for j in range(L)]
    lane_of = [jnp.maximum(shift[j] - 1, 0) for j in range(L)]
    in_slot = [
        lax.rem(moves[lax.rem(me - shift[j] + R, R) * L + j, 1], S) for j in range(L)
    ]

    def pick(values, k):
        found = values[0]
        for j in range(1, L):
            found = jnp.where(shift[j] == k, values[j], found)
        return found

    def source(g):
        row, lane = g, 0
        for j in range(L):
            hit = in_slot[j] == g
            row = jnp.where(hit, S + j, row)
            lane = jnp.where(hit, lane_of[j], lane)
        return row, lane

    def lane_copy(src, dst, send, recv, k, forward=True):
        to = lax.rem(me + k, R) if forward else lax.rem(me - k + R, R)
        return pltpu.make_async_remote_copy(
            src_ref=src.at[k - 1],
            dst_ref=dst.at[k - 1],
            send_sem=send.at[k - 1],
            recv_sem=recv.at[k - 1],
            device_id={"replica": to},
            device_id_type=MESH,
        )

    ask_copy = lambda k: lane_copy(send_ask, got_ask, ask_s, ask_r, k, False)
    small_copy = lambda k: lane_copy(send_small, got_small, small_s, small_r, k)
    state_copy = lambda k: lane_copy(send_state, got_state, state_s, state_r, k)
    att_copy = lambda k: lane_copy(send_att, got_att, att_s, att_r, k)

    pl.semaphore_wait(barrier, R - 1 + T - 1)

    def send_first(k, _):
        send_ask[k - 1] = asks[1, pick(in_slot, k)]
        ask_copy(k).start()
        send_small[k - 1] = small[pick(out_slot, k)]
        small_copy(k).start()
        return 0

    lax.fori_loop(1, R, send_first, 0)
    loads[0].wait()

    def send_states(k, _):
        slot = pick(out_slot, k)
        for c in chunks(C):
            send_state[k - 1, :, c] = h[slot, :, c].astype(BF16)
        state_copy(k).start()
        return 0

    lax.fori_loop(1, R, send_states, 0)

    for g in range(S):
        row, lane = source(g)
        table[g] = row
        table[S + g] = lane

    loads[1].wait()
    loads[2].wait()
    lax.fori_loop(1, R, lambda k, _: (ask_copy(k).wait(), 0)[1], 0)

    rows = 2 * H
    head_of = lax.broadcasted_iota(jnp.int32, (rows, 1), 0) % H // (H // KV)
    step_of = lax.broadcasted_iota(jnp.int32, (rows, 1), 0) // H
    ask_col = lax.broadcasted_iota(jnp.int32, (rows, asks.shape[2]), 1)
    pos = lax.broadcasted_iota(jnp.int32, (rows, n_pages * page), 1)
    is_key = ask_col == H + head_of
    is_val = ask_col == H + KV + head_of
    nt = (((1,), (1,)), ((), ()))
    nn = (((1,), (0,)), ((), ()))

    def attend(g, _):
        length = lengths[me * S + g]
        gone = jnp.int32(0)
        lane = jnp.int32(0)
        for j in range(L):
            hit = out_slot[j] == g
            gone = jnp.where(hit, 1, gone)
            lane = jnp.where(hit, lane_of[j], lane)
        one = asks[0, g]
        two = jnp.where(gone == 1, got_ask[lane].astype(F32), asks[1, g].astype(F32)).astype(BF16)
        q = jnp.concatenate([one.astype(F32)[:H], two.astype(F32)[:H]], axis=0)
        qb = q.astype(BF16)
        wide = jnp.concatenate(
            [jnp.where(head_of == i, q, 0.0) for i in range(KV)], axis=1
        ).astype(BF16)
        scores = jnp.concatenate(
            [
                lax.dot_general(wide, keys[pages[g, p]], nt, preferred_element_type=F32)
                for p in range(n_pages)
            ],
            axis=1,
        )
        new_one = lax.dot_general(qb, one, nt, preferred_element_type=F32)
        new_two = lax.dot_general(qb, two, nt, preferred_element_type=F32)
        new_one = jnp.sum(jnp.where(is_key, new_one, 0.0), axis=1, keepdims=True)
        new_two = jnp.sum(jnp.where(is_key, new_two, 0.0), axis=1, keepdims=True)
        at_one, at_two = pos == length, pos == length + 1
        scores = jnp.where(at_one, new_one, jnp.where(at_two, new_two, scores))
        scores = scores * (1.0 / math.sqrt(HD))
        scores = jnp.where(pos <= length + step_of, scores, -1e30)
        expo = jnp.exp(scores - jnp.max(scores, axis=1, keepdims=True))
        w = expo / jnp.sum(expo, axis=1, keepdims=True)
        w_one = jnp.sum(jnp.where(at_one, w, 0.0), axis=1, keepdims=True)
        w_two = jnp.sum(jnp.where(at_two, w, 0.0), axis=1, keepdims=True)
        w = jnp.where(at_one | at_two, 0.0, w).astype(BF16)
        mixed = lax.dot_general(
            w[:, :page], vals[pages[g, 0]], nn, preferred_element_type=F32
        )
        for p in range(1, n_pages):
            mixed += lax.dot_general(
                w[:, p * page : (p + 1) * page],
                vals[pages[g, p]],
                nn,
                preferred_element_type=F32,
            )
        out = lax.dot_general(
            jnp.where(is_val, w_one, 0.0).astype(BF16), one, nn, preferred_element_type=F32
        ) + lax.dot_general(
            jnp.where(is_val, w_two, 0.0).astype(BF16), two, nn, preferred_element_type=F32
        )
        for i in range(KV):
            out += jnp.where(head_of == i, mixed[:, i * HD : (i + 1) * HD], 0.0)
        first, second = out[:H], out[H:]
        if att.shape[2] > H:
            pad = jnp.zeros((att.shape[2] - H, HD), F32)
            first = jnp.concatenate([first, pad], axis=0)
            second = jnp.concatenate([second, pad], axis=0)
        att[0, g] = first.astype(BF16)
        att_two[g] = second.astype(BF16)
        return 0

    lax.fori_loop(0, S, attend, 0, unroll=2)

    def send_back(k, _):
        send_att[k - 1] = att_two[pick(out_slot, k)]
        att_copy(k).start()
        return 0

    lax.fori_loop(1, R, send_back, 0)

    for k in range(3):
        win[k, :S] = conv[k]
    win[3, :S] = mx[0].astype(F32)
    lax.fori_loop(1, R, lambda k, _: (small_copy(k).wait(), 0)[1], 0)
    for j in range(L):
        tile = got_small[lane_of[j]].astype(F32)
        for k in range(4):
            win[k, S + j : S + j + 1] = jnp.concatenate(
                [tile[4 * k + i : 4 * k + i + 1] for i in range(4)], axis=1
            )
    for k in range(4):
        win[k, S + L :] = jnp.zeros((NR - S - L, C), F32)

    def project(src, n, xc_ref, buf):
        low = jnp.zeros((n, rank), F32)
        bc = jnp.zeros((n, bc_w.shape[1]), F32)
        for c in chunks(C):
            total = conv_b[:, c] + src(0, c) * conv_w[0:1, c]
            for k in range(1, 4):
                total += src(k, c) * conv_w[k : k + 1, c]
            xb = silu(total).astype(BF16)
            xc_ref[:, c] = xb.astype(F32)
            low += lax.dot_general(xb, down[c], nn, preferred_element_type=F32)
            bc += lax.dot_general(xb, bc_w[c], nn, preferred_element_type=F32)
        buf[core, :, :rank] = low
        buf[core, :, rank:] = jnp.concatenate(
            [bc, jnp.zeros((n, HD - bc.shape[1]), F32)], axis=1
        )

    def core_copy(buf, which, k):
        return pltpu.make_async_remote_copy(
            src_ref=buf.at[core],
            dst_ref=buf.at[core],
            send_sem=part_s.at[which, k],
            recv_sem=part_r.at[which, k],
            device_id={"tensor": lax.rem(core + k, T)},
            device_id_type=MESH,
        )

    def reduce_parts(buf, which):
        lax.fori_loop(1, T, lambda k, _: (core_copy(buf, which, k).start(), 0)[1], 0)
        lax.fori_loop(1, T, lambda k, _: (core_copy(buf, which, k).wait(), 0)[1], 0)
        total = buf[0]
        for t in range(1, T):
            total += buf[t]
        return total

    def steps(total, n, dt_ref, b_ref, c_ref):
        low = total[:, :rank].astype(BF16)
        for c in chunks(C):
            dt_ref[:, c] = softplus(
                lax.dot_general(low, up[:, c], nn, preferred_element_type=F32) + dt_b[:, c]
            )
        turned = total[:, rank : rank + HD].T
        for i in range(n):
            b_ref[i] = jnp.broadcast_to(turned[:N, i : i + 1], (N, HD))
            c_ref[i] = jnp.broadcast_to(turned[N : 2 * N, i : i + 1], (N, HD))

    loads[3].wait()
    loads[4].wait()
    loads[5].wait()
    project(lambda k, c: win[k, :, c], NR, xc_all, part)
    steps(reduce_parts(part, 0), NR, dt_all, b_all, c_all)
    dt_moved[...] = dt_all[S:]
    xc_moved[...] = xc_all[S:]
    b_moved[...] = b_all[S:]

    for g in range(S):
        row, _ = source(g)
        for k in range(3):
            win_two[k, g : g + 1] = win[k + 1, pl.ds(row, 1), :]
    win_two[3] = mx[1].astype(F32)
    for k in range(3):
        fconv[k] = win_two[k + 1]
    project(lambda k, c: win_two[k, :, c], S, xc_two, part_two)
    steps(reduce_parts(part_two, 1), S, dt_two, b_two, c_two)

    def scan(g, _):
        reps = 512 // HD if C >= 512 else C // HD
        b = jnp.concatenate([b_all[g]] * reps, axis=1)
        cc = jnp.concatenate([c_all[g]] * reps, axis=1)
        for c in chunks(C):
            dt = dt_all[pl.ds(g, 1), c]
            x = xc_all[pl.ds(g, 1), c]
            new = jnp.exp(-dt * jnp.exp(a_log[:, c])) * h[g, :, c] + b * (dt * x)
            h[g, :, c] = new
            y[pl.ds(g, 1), c] = jnp.sum(cc * new, axis=0, keepdims=True)
        return 0

    lax.fori_loop(0, S, scan, 0)
    save = pltpu.make_async_copy(h, state_one, load_sem.at[0])
    save.start()
    for c in chunks(C):
        m_one[:, c] = (
            (y[:, c] + skip[:, c] * xc_all[:S, c]) * silu(mz[0, :, c].astype(F32))
        ).astype(BF16)

    lax.fori_loop(1, R, lambda k, _: (att_copy(k).wait(), 0)[1], 0)
    for g in range(S):
        row, lane = source(g)
        att[1, g] = jnp.where(
            row >= S, got_att[lane].astype(F32), att_two[g].astype(F32)
        ).astype(BF16)
    save.wait()
    lax.fori_loop(1, R, lambda k, _: (state_copy(k).wait(), 0)[1], 0)


def finish_kernel(
    sizes,
    table,
    kept,
    arrived,
    dt_moved,
    xc_moved,
    b_moved,
    dt_two,
    xc_two,
    b_two,
    c_two,
    a_log,
    skip,
    mz,
    m_one,
    final,
    out,
    rate,
    y,
):
    S = sizes
    C = final.shape[2]
    g = pl.program_id(0)
    row = table[g]
    reps = min(512, C) // HD

    @pl.when(g == 0)
    def _():
        rate[...] = jnp.exp(a_log[...])
        out[0] = m_one[...]

    wide = lambda v: jnp.concatenate([v] * reps, axis=1)

    def second(prev, c):
        dt, x = dt_two[pl.ds(g, 1), c], xc_two[pl.ds(g, 1), c]
        new = jnp.exp(-dt * rate[:, c]) * prev + wide(b_two[g]) * (dt * x)
        final[0, :, c] = new
        y[pl.ds(g, 1), c] = jnp.sum(wide(c_two[g]) * new, axis=0, keepdims=True)

    @pl.when(row < S)
    def _():
        for c in chunks(C):
            second(kept[0, :, c], c)

    @pl.when(row >= S)
    def _():
        j = row - S
        for c in chunks(C):
            dt, x = dt_moved[pl.ds(j, 1), c], xc_moved[pl.ds(j, 1), c]
            one = jnp.exp(-dt * rate[:, c]) * arrived[0, :, c].astype(F32)
            second(one + wide(b_moved[j]) * (dt * x), c)

    @pl.when(g == S - 1)
    def _():
        for c in chunks(C):
            out[1, :, c] = (
                (y[:, c] + skip[:, c] * xc_two[:, c]) * silu(mz[1, :, c].astype(F32))
            ).astype(BF16)


def shards(
    lengths,
    page_table,
    key_pool,
    value_pool,
    queries,
    new_keys,
    new_values,
    conv_state,
    ssm_state,
    mamba_x,
    mamba_z,
    conv_weight,
    conv_bias,
    dt_down,
    bc_proj,
    dt_up,
    dt_bias,
    a_log,
    skip_d,
    moves,
):
    R, T = lax.axis_size("replica"), lax.axis_size("tensor")
    S, N, C = ssm_state.shape
    L = moves.shape[0] // R
    QW, W = queries.shape[2], key_pool.shape[2]
    H, KV = QW // HD, W // HD
    A = round_up(H + 2 * KV, 16)
    AH = round_up(H, 16)
    NR = S + round_up(L, 16)
    rank = dt_down.shape[1]

    heads = lambda t: t.reshape(2, S, -1, HD)
    asks = jnp.concatenate(
        [
            heads(queries),
            heads(new_keys),
            heads(new_values),
            jnp.zeros((2, S, A - H - 2 * KV, HD), BF16),
        ],
        axis=2,
    )
    small = jnp.concatenate(
        [conv_state.astype(BF16), mamba_x[0][:, None]], axis=1
    ).reshape(S, 16, C // 4)
    conv = jnp.transpose(conv_state, (1, 0, 2))
    row = lambda v: v.reshape(1, C)
    shape = jax.ShapeDtypeStruct
    dma = pltpu.SemaphoreType.DMA
    outs = pl.pallas_call(
        functools.partial(exchange_kernel, (R, T, S, L, H, KV)),
        out_shape=(
            shape((S, N, C), F32),
            shape((R - 1, N, C), BF16),
            shape((2, S, AH, HD), BF16),
            shape((3, S, C), F32),
            shape((S, C), BF16),
            shape((NR - S, C), F32),
            shape((NR - S, C), F32),
            shape((NR - S, N, HD), F32),
            shape((S, C), F32),
            shape((S, C), F32),
            shape((S, N, HD), F32),
            shape((S, N, HD), F32),
            shape((2 * S,), jnp.int32),
        ),
        in_specs=[SMEM, SMEM, SMEM, ANY, ANY, VMEM, VMEM, ANY]
        + [VMEM] * 5
        + [ANY] * 3
        + [VMEM] * 3,
        out_specs=(ANY, ANY) + (VMEM,) * 10 + (SMEM,),
        scratch_shapes=[
            pltpu.VMEM(key_pool.shape, BF16),
            pltpu.VMEM(value_pool.shape, BF16),
            pltpu.VMEM((S, N, C), F32),
            pltpu.VMEM(dt_down.shape, BF16),
            pltpu.VMEM(bc_proj.shape, BF16),
            pltpu.VMEM(dt_up.shape, BF16),
            pltpu.VMEM((R - 1, N, C), BF16),
            pltpu.VMEM((R - 1, 16, C // 4), BF16),
            pltpu.VMEM((R - 1, 16, C // 4), BF16),
            pltpu.VMEM((R - 1, A, HD), BF16),
            pltpu.VMEM((R - 1, A, HD), BF16),
            pltpu.VMEM((S, AH, HD), BF16),
            pltpu.VMEM((R - 1, AH, HD), BF16),
            pltpu.VMEM((R - 1, AH, HD), BF16),
            pltpu.VMEM((4, NR, C), F32),
            pltpu.VMEM((4, S, C), F32),
            pltpu.VMEM((NR, C), F32),
            pltpu.VMEM((NR, C), F32),
            pltpu.VMEM((NR, N, HD), F32),
            pltpu.VMEM((NR, N, HD), F32),
            pltpu.VMEM((S, C), F32),
            pltpu.VMEM((T, NR, rank + HD), F32),
            pltpu.VMEM((T, S, rank + HD), F32),
            dma((6,)),
        ]
        + [dma((R - 1,))] * 8
        + [dma((2, T))] * 2,
        compiler_params=pltpu.CompilerParams(
            collective_id=0, has_side_effects=True, vmem_limit_bytes=48 * 1024 * 1024
        ),
        name="exchange",
    )(
        moves,
        lengths,
        page_table,
        key_pool,
        value_pool,
        asks,
        small,
        ssm_state,
        conv,
        mamba_x,
        mamba_z,
        conv_weight,
        row(conv_bias),
        dt_down,
        bc_proj,
        dt_up,
        row(dt_bias),
        a_log,
        row(skip_d),
    )
    state_one, got_state, att, fconv, m_one = outs[:5]
    table = outs[12]
    whole = lambda v: pl.BlockSpec(v.shape, lambda g, t: (0,) * v.ndim)
    rest = list(outs[5:12]) + [a_log, row(skip_d), mamba_z, m_one]
    final_ssm, mamba_out = pl.pallas_call(
        functools.partial(finish_kernel, S),
        grid_spec=pltpu.PrefetchScalarGridSpec(
            num_scalar_prefetch=1,
            grid=(S,),
            in_specs=[
                pl.BlockSpec((1, N, C), lambda g, t: (g, 0, 0)),
                pl.BlockSpec((1, N, C), lambda g, t: (t[S + g], 0, 0)),
            ]
            + [whole(v) for v in rest],
            out_specs=[
                pl.BlockSpec((1, N, C), lambda g, t: (g, 0, 0)),
                pl.BlockSpec((2, S, C), lambda g, t: (0, 0, 0)),
            ],
            scratch_shapes=[pltpu.VMEM((N, C), F32), pltpu.VMEM((S, C), F32)],
        ),
        out_shape=(shape((S, N, C), F32), shape((2, S, C), BF16)),
        compiler_params=pltpu.CompilerParams(vmem_limit_bytes=32 * 1024 * 1024),
        name="finish",
    )(table, state_one, got_state, *rest)
    return (
        att[:, :, :H].reshape(2, S, QW),
        mamba_out,
        final_ssm,
        jnp.transpose(fconv, (1, 0, 2)),
    )


def solution(mesh):
    row, both = P("replica", None, "tensor"), P(None, "replica", "tensor")
    in_specs = (
        P(),
        P("replica", None),
        row,
        row,
        both,
        both,
        both,
        row,
        row,
        both,
        both,
        P(None, "tensor"),
        P("tensor"),
        P("tensor", None),
        P("tensor", None),
        P(None, "tensor"),
        P("tensor"),
        P(None, "tensor"),
        P("tensor"),
        P(),
    )
    return jax.shard_map(
        shards, mesh=mesh, in_specs=in_specs, out_specs=(both, both, row, row), check_vma=False
    )
```

```python
import functools
import math

import jax
import jax.numpy as jnp
from jax import lax
from jax.experimental import pallas as pl
from jax.experimental.pallas import tpu as pltpu
from jax.sharding import PartitionSpec as P

HD = 128
F32, BF16 = jnp.float32, jnp.bfloat16
MESH = pl.DeviceIdType.MESH
ANY = pl.BlockSpec(memory_space=pl.ANY)
SMEM = pl.BlockSpec(memory_space=pltpu.SMEM)


def round_up(n, m):
    return (n + m - 1) // m * m


def silu(v):
    return v / (1.0 + jnp.exp(-v))


def softplus(v):
    return jnp.maximum(v, 0.0) + jnp.log1p(jnp.exp(-jnp.abs(v)))


def chunks(total, most=512):
    step = min(most, total)
    return [slice(i, i + step) for i in range(0, total, step)]


def exchange_kernel(
    sizes,
    moves,
    lengths,
    pages,
    conv_hbm,
    mx_hbm,
    q_hbm,
    nk_hbm,
    nv_hbm,
    states_hbm,
    keys_hbm,
    vals_hbm,
    conv_w_hbm,
    conv_b_hbm,
    down_hbm,
    bc_hbm,
    up_hbm,
    dt_b_hbm,
    a_log_hbm,
    skip_hbm,
    mz_hbm,
    state_one,
    got_state,
    att_out,
    fconv,
    m_one,
    vec_moved,
    b_moved,
    vec_two,
    bc_two,
    win,
    mx,
    queries,
    nk,
    nv,
    h,
    keys,
    vals,
    conv_w,
    conv_b,
    down,
    bc_w,
    up,
    dt_b,
    a_log,
    skip,
    mz,
    flat,
    asks,
    pack,
    send_state,
    send_small,
    got_small,
    send_ask,
    got_ask,
    att,
    att_two,
    send_att,
    got_att,
    win_two,
    xc_all,
    dt_all,
    b_all,
    c_all,
    xc_two,
    dt_two,
    b_two,
    c_two,
    rate,
    y,
    m_buf,
    part,
    part_two,
    load_sem,
    save_sem,
    state_s,
    state_r,
    small_s,
    small_r,
    ask_s,
    ask_r,
    att_s,
    att_r,
    part_s,
    part_r,
):
    R, T, S, L, H, KV = sizes
    C = h.shape[2]
    N = a_log.shape[0]
    NR = win.shape[1]
    rank = down.shape[1]
    page = keys.shape[1]
    n_pages = pages.shape[0]
    QW, W = queries.shape[2], keys.shape[2]
    A = asks.shape[2]
    me = lax.axis_index("replica")
    core = lax.axis_index("tensor")

    pairs = [(conv_hbm.at[k], win.at[k, pl.ds(0, S)]) for k in range(3)] + [
        (mx_hbm, mx),
        (q_hbm, queries),
        (nk_hbm, nk),
        (nv_hbm, nv),
        (states_hbm, h),
        (keys_hbm, keys),
        (vals_hbm, vals),
        (conv_w_hbm, conv_w),
        (conv_b_hbm, conv_b),
        (down_hbm, down),
        (bc_hbm, bc_w),
        (up_hbm, up),
        (dt_b_hbm, dt_b),
        (a_log_hbm, a_log),
        (skip_hbm, skip),
        (mz_hbm, mz),
    ]
    loads = [
        pltpu.make_async_copy(src, dst, load_sem.at[i]) for i, (src, dst) in enumerate(pairs)
    ]
    for load in loads:
        load.start()
    saves = []

    def save(src, dst):
        copy = pltpu.make_async_copy(src, dst, save_sem.at[len(saves)])
        copy.start()
        saves.append(copy)

    barrier = pltpu.get_barrier_semaphore()

    def greet(k, _):
        pl.semaphore_signal(
            barrier, inc=1, device_id={"replica": lax.rem(me + k, R)}, device_id_type=MESH
        )
        return 0

    def greet_core(k, _):
        pl.semaphore_signal(
            barrier, inc=1, device_id={"tensor": lax.rem(core + k, T)}, device_id_type=MESH
        )
        return 0

    lax.fori_loop(1, R, greet, 0)
    lax.fori_loop(1, T, greet_core, 0)

    shift = [lax.div(moves[1, j], S) for j in range(L)]
    out_slot = [lax.rem(moves[0, me * L + j], S) for j in range(L)]
    lane_of = [jnp.maximum(shift[j] - 1, 0) for j in range(L)]
    in_slot = [
        lax.rem(moves[1, lax.rem(me - shift[j] + R, R) * L + j], S) for j in range(L)
    ]

    def pick(values, k):
        found = values[0]
        for j in range(1, L):
            found = jnp.where(shift[j] == k, values[j], found)
        return found

    def source(g):
        row, lane = g, 0
        for j in range(L):
            hit = in_slot[j] == g
            row = jnp.where(hit, S + j, row)
            lane = jnp.where(hit, lane_of[j], lane)
        return row, lane

    def lane_copy(src, dst, send, recv, k, forward=True):
        to = lax.rem(me + k, R) if forward else lax.rem(me - k + R, R)
        return pltpu.make_async_remote_copy(
            src_ref=src.at[k - 1],
            dst_ref=dst.at[k - 1],
            send_sem=send.at[k - 1],
            recv_sem=recv.at[k - 1],
            device_id={"replica": to},
            device_id_type=MESH,
        )

    ask_copy = lambda k: lane_copy(send_ask, got_ask, ask_s, ask_r, k, False)
    small_copy = lambda k: lane_copy(send_small, got_small, small_s, small_r, k)
    state_copy = lambda k: lane_copy(send_state, got_state, state_s, state_r, k)
    att_copy = lambda k: lane_copy(send_att, got_att, att_s, att_r, k)

    for load in loads[4:7]:
        load.wait()
    for t in range(2):
        flat[t, :, :QW] = queries[t].astype(F32)
        flat[t, :, QW : QW + W] = nk[t].astype(F32)
        flat[t, :, QW + W :] = nv[t].astype(F32)

    def tile_up(g, _):
        for t in range(2):
            line = flat[t, pl.ds(g, 1), :]
            parts = [line[:, i * HD : (i + 1) * HD] for i in range(H + 2 * KV)]
            if A > H + 2 * KV:
                parts.append(jnp.zeros((A - H - 2 * KV, HD), F32))
            asks[t, g] = jnp.concatenate(parts, axis=0).astype(BF16)
        return 0

    lax.fori_loop(0, S, tile_up, 0)

    for load in loads[:4]:
        load.wait()
    win[3, :S] = mx[0].astype(F32)
    for j in range(L):
        lines = [win[k, pl.ds(out_slot[j], 1), :] for k in range(4)]
        pack[j] = jnp.concatenate(
            [line[:, i * (C // 4) : (i + 1) * (C // 4)] for line in lines for i in range(4)],
            axis=0,
        ).astype(BF16)

    pl.semaphore_wait(barrier, R - 1 + T - 1)

    def send_first(k, _):
        send_ask[k - 1] = asks[1, pick(in_slot, k)]
        ask_copy(k).start()
        send_small[k - 1] = pack[pick(range(L), k)]
        small_copy(k).start()
        return 0

    lax.fori_loop(1, R, send_first, 0)
    loads[7].wait()

    def send_states(k, _):
        slot = pick(out_slot, k)
        for c in chunks(C):
            send_state[k - 1, :, c] = h[slot, :, c].astype(BF16)
        state_copy(k).start()
        return 0

    lax.fori_loop(1, R, send_states, 0)

    loads[8].wait()
    loads[9].wait()
    lax.fori_loop(1, R, lambda k, _: (ask_copy(k).wait(), 0)[1], 0)

    rows = 2 * H
    head_of = lax.broadcasted_iota(jnp.int32, (rows, 1), 0) % H // (H // KV)
    step_of = lax.broadcasted_iota(jnp.int32, (rows, 1), 0) // H
    ask_col = lax.broadcasted_iota(jnp.int32, (rows, asks.shape[2]), 1)
    pos = lax.broadcasted_iota(jnp.int32, (rows, n_pages * page), 1)
    is_key = ask_col == H + head_of
    is_val = ask_col == H + KV + head_of
    nt = (((1,), (1,)), ((), ()))
    nn = (((1,), (0,)), ((), ()))

    def attend(g):
        length = lengths[me * S + g]
        gone = jnp.int32(0)
        lane = jnp.int32(0)
        for j in range(L):
            hit = out_slot[j] == g
            gone = jnp.where(hit, 1, gone)
            lane = jnp.where(hit, lane_of[j], lane)
        one = asks[0, g]
        two = jnp.where(gone == 1, got_ask[lane].astype(F32), asks[1, g].astype(F32)).astype(BF16)
        q = jnp.concatenate([one.astype(F32)[:H], two.astype(F32)[:H]], axis=0)
        qb = q.astype(BF16)
        wide = jnp.concatenate(
            [jnp.where(head_of == i, q, 0.0) for i in range(KV)], axis=1
        ).astype(BF16)
        scores = jnp.concatenate(
            [
                lax.dot_general(wide, keys[pages[p, g]], nt, preferred_element_type=F32)
                for p in range(n_pages)
            ],
            axis=1,
        )
        new_one = lax.dot_general(qb, one, nt, preferred_element_type=F32)
        new_two = lax.dot_general(qb, two, nt, preferred_element_type=F32)
        new_one = jnp.sum(jnp.where(is_key, new_one, 0.0), axis=1, keepdims=True)
        new_two = jnp.sum(jnp.where(is_key, new_two, 0.0), axis=1, keepdims=True)
        at_one, at_two = pos == length, pos == length + 1
        scores = jnp.where(at_one, new_one, jnp.where(at_two, new_two, scores))
        scores = scores * (1.0 / math.sqrt(HD))
        scores = jnp.where(pos <= length + step_of, scores, -1e30)
        expo = jnp.exp(scores - jnp.max(scores, axis=1, keepdims=True))
        w = expo / jnp.sum(expo, axis=1, keepdims=True)
        w_one = jnp.sum(jnp.where(at_one, w, 0.0), axis=1, keepdims=True)
        w_two = jnp.sum(jnp.where(at_two, w, 0.0), axis=1, keepdims=True)
        w = jnp.where(at_one | at_two, 0.0, w).astype(BF16)
        mixed = lax.dot_general(
            w[:, :page], vals[pages[0, g]], nn, preferred_element_type=F32
        )
        for p in range(1, n_pages):
            mixed += lax.dot_general(
                w[:, p * page : (p + 1) * page],
                vals[pages[p, g]],
                nn,
                preferred_element_type=F32,
            )
        out = lax.dot_general(
            jnp.where(is_val, w_one, 0.0).astype(BF16), one, nn, preferred_element_type=F32
        ) + lax.dot_general(
            jnp.where(is_val, w_two, 0.0).astype(BF16), two, nn, preferred_element_type=F32
        )
        for i in range(KV):
            out += jnp.where(head_of == i, mixed[:, i * HD : (i + 1) * HD], 0.0)
        first, second = out[:H], out[H:]
        if att.shape[2] > H:
            pad = jnp.zeros((att.shape[2] - H, HD), F32)
            first = jnp.concatenate([first, pad], axis=0)
            second = jnp.concatenate([second, pad], axis=0)
        return first.astype(BF16), second.astype(BF16)

    batch = 4 if S % 4 == 0 else 1

    def attend_some(i, _):
        results = [attend(i * batch + b) for b in range(batch)]
        for b, (first, second) in enumerate(results):
            att[0, i * batch + b] = first
            att_two[i * batch + b] = second
        return 0

    lax.fori_loop(0, S // batch, attend_some, 0)

    def send_back(k, _):
        send_att[k - 1] = att_two[pick(out_slot, k)]
        att_copy(k).start()
        return 0

    lax.fori_loop(1, R, send_back, 0)

    lax.fori_loop(1, R, lambda k, _: (small_copy(k).wait(), 0)[1], 0)
    for j in range(L):
        tile = got_small[lane_of[j]].astype(F32)
        for k in range(4):
            win[k, S + j : S + j + 1] = jnp.concatenate(
                [tile[4 * k + i : 4 * k + i + 1] for i in range(4)], axis=1
            )
    for k in range(4):
        win[k, S + L :] = jnp.zeros((NR - S - L, C), F32)

    def project(src, n, xc_ref, buf):
        low = jnp.zeros((n, rank), F32)
        bc = jnp.zeros((n, bc_w.shape[0]), F32)
        for c in chunks(C):
            total = conv_b[:, c] + src(0, c) * conv_w[0:1, c]
            for k in range(1, 4):
                total += src(k, c) * conv_w[k : k + 1, c]
            xb = silu(total).astype(BF16)
            xc_ref[:, c] = xb.astype(F32)
            low += lax.dot_general(xb, down[c], nn, preferred_element_type=F32)
            bc += lax.dot_general(xb, bc_w[:, c], nt, preferred_element_type=F32)
        buf[core, :, :rank] = low
        buf[core, :, rank:] = jnp.concatenate(
            [bc, jnp.zeros((n, HD - bc.shape[1]), F32)], axis=1
        )

    def core_copy(buf, which, k):
        return pltpu.make_async_remote_copy(
            src_ref=buf.at[core],
            dst_ref=buf.at[core],
            send_sem=part_s.at[which, k],
            recv_sem=part_r.at[which, k],
            device_id={"tensor": lax.rem(core + k, T)},
            device_id_type=MESH,
        )

    def reduce_parts(buf, which):
        lax.fori_loop(1, T, lambda k, _: (core_copy(buf, which, k).start(), 0)[1], 0)
        lax.fori_loop(1, T, lambda k, _: (core_copy(buf, which, k).wait(), 0)[1], 0)
        total = buf[0]
        for t in range(1, T):
            total += buf[t]
        return total

    def steps(total, n, dt_ref, b_ref, c_ref):
        low = total[:, :rank].astype(BF16)
        for c in chunks(C):
            dt_ref[:, c] = softplus(
                lax.dot_general(low, up[:, c], nn, preferred_element_type=F32) + dt_b[:, c]
            )
        turned = total[:, rank : rank + HD].T
        for i in range(n):
            b_ref[i] = jnp.broadcast_to(turned[:N, i : i + 1], (N, HD))
            c_ref[i] = jnp.broadcast_to(turned[N : 2 * N, i : i + 1], (N, HD))

    for load in loads[10:]:
        load.wait()
    rate[...] = jnp.exp(a_log[...])
    project(lambda k, c: win[k, :, c], NR, xc_all, part)
    steps(reduce_parts(part, 0), NR, dt_all, b_all, c_all)
    moved = pl.ds(S, NR - S)
    save(dt_all.at[moved], vec_moved.at[0])
    save(xc_all.at[moved], vec_moved.at[1])
    save(b_all.at[moved], b_moved)

    for g in range(S):
        row, _ = source(g)
        for k in range(3):
            win_two[k, g : g + 1] = win[k + 1, pl.ds(row, 1), :]
    win_two[3] = mx[1].astype(F32)
    save(win_two.at[pl.ds(1, 3)], fconv)
    project(lambda k, c: win_two[k, :, c], S, xc_two, part_two)
    steps(reduce_parts(part_two, 1), S, dt_two, b_two, c_two)
    save(dt_two, vec_two.at[0])
    save(xc_two, vec_two.at[1])
    save(b_two, bc_two.at[0])
    save(c_two, bc_two.at[1])

    def scan(g, _):
        for c in chunks(C, 2048):
            reps = (c.stop - c.start) // HD
            dt = dt_all[pl.ds(g, 1), c]
            x = xc_all[pl.ds(g, 1), c]
            new = jnp.exp(-dt * rate[:, c]) * h[g, :, c]
            new += jnp.concatenate([b_all[g]] * reps, axis=1) * (dt * x)
            line = jnp.sum(jnp.concatenate([c_all[g]] * reps, axis=1) * new, axis=0, keepdims=True)
            h[g, :, c] = new
            y[pl.ds(g, 1), c] = line
        return 0

    lax.fori_loop(0, S, scan, 0)
    save(h, state_one)
    for c in chunks(C):
        m_buf[:, c] = (
            (y[:, c] + skip[:, c] * xc_all[:S, c]) * silu(mz[0, :, c].astype(F32))
        ).astype(BF16)

    save(m_buf, m_one)

    lax.fori_loop(1, R, lambda k, _: (att_copy(k).wait(), 0)[1], 0)
    for g in range(S):
        row, lane = source(g)
        att[1, g] = jnp.where(
            row >= S, got_att[lane].astype(F32), att_two[g].astype(F32)
        ).astype(BF16)
    save(att, att_out)
    for copy in saves:
        copy.wait()
    lax.fori_loop(1, R, lambda k, _: (state_copy(k).wait(), 0)[1], 0)


def arrival(moves, me, g, R, S, L):
    row, lane = g, 0
    for j in range(L):
        shift = lax.div(moves[1, j], S)
        slot = lax.rem(moves[1, lax.rem(me - shift + R, R) * L + j], S)
        row = jnp.where(slot == g, S + j, row)
        lane = jnp.where(slot == g, jnp.maximum(shift - 1, 0), lane)
    return row, lane


def finish_kernel(
    sizes,
    moves,
    here,
    kept,
    arrived,
    vec_moved,
    b_moved,
    vec_two,
    bc_two,
    a_log,
    skip,
    mz,
    m_one,
    final,
    out,
    rate,
    y,
):
    R, S, L = sizes
    C = final.shape[2]
    g = pl.program_id(0)
    row, _ = arrival(moves, here[0], g, R, S, L)
    wide = lambda v, c: jnp.concatenate([v] * ((c.stop - c.start) // HD), axis=1)

    @pl.when(g == 0)
    def _():
        rate[...] = jnp.exp(a_log[...])
        out[0] = m_one[...]

    def second(prev, c):
        dt, x = vec_two[0, pl.ds(g, 1), c], vec_two[1, pl.ds(g, 1), c]
        new = jnp.exp(-dt * rate[:, c]) * prev + wide(bc_two[0, g], c) * (dt * x)
        line = jnp.sum(wide(bc_two[1, g], c) * new, axis=0, keepdims=True)
        final[0, :, c] = new
        y[pl.ds(g, 1), c] = line

    @pl.when(row < S)
    def _():
        for c in chunks(C, 2048):
            second(kept[0, :, c], c)

    @pl.when(row >= S)
    def _():
        j = row - S
        for c in chunks(C, 2048):
            dt, x = vec_moved[0, pl.ds(j, 1), c], vec_moved[1, pl.ds(j, 1), c]
            one = jnp.exp(-dt * rate[:, c]) * arrived[0, :, c].astype(F32)
            second(one + wide(b_moved[j], c) * (dt * x), c)

    @pl.when(g == S - 1)
    def _():
        for c in chunks(C):
            out[1, :, c] = (
                (y[:, c] + skip[:, c] * vec_two[1, :, c]) * silu(mz[1, :, c].astype(F32))
            ).astype(BF16)


def shards(
    lengths,
    page_table,
    key_pool,
    value_pool,
    queries,
    new_keys,
    new_values,
    conv_state,
    ssm_state,
    mamba_x,
    mamba_z,
    conv_weight,
    conv_bias,
    dt_down,
    bc_proj,
    dt_up,
    dt_bias,
    a_log,
    skip_d,
    moves,
):
    R, T = lax.axis_size("replica"), lax.axis_size("tensor")
    S, N, C = ssm_state.shape
    L = moves.shape[0] // R
    QW, W = queries.shape[2], key_pool.shape[2]
    H, KV = QW // HD, W // HD
    A = round_up(H + 2 * KV, 16)
    AH = round_up(H, 16)
    NR = S + round_up(L, 16)
    rank = dt_down.shape[1]

    row = lambda v: v.reshape(1, C)
    shape = jax.ShapeDtypeStruct
    dma = pltpu.SemaphoreType.DMA
    vm = lambda dims, kind=F32: pltpu.VMEM(dims, kind)
    like = lambda v: pltpu.VMEM(v.shape, v.dtype)
    NM = NR - S
    turned = moves.T
    operands = (
        jnp.transpose(conv_state, (1, 0, 2)),
        mamba_x,
        queries,
        new_keys,
        new_values,
        ssm_state,
        key_pool,
        value_pool,
        conv_weight,
        row(conv_bias),
        dt_down,
        bc_proj.T,
        dt_up,
        row(dt_bias),
        a_log,
        row(skip_d),
        mamba_z,
    )
    state_one, got_state, att, fconv, m_one, *rest = pl.pallas_call(
        functools.partial(exchange_kernel, (R, T, S, L, H, KV)),
        out_shape=(
            shape((S, N, C), F32),
            shape((R - 1, N, C), BF16),
            shape((2, S, AH, HD), BF16),
            shape((3, S, C), F32),
            shape((S, C), BF16),
            shape((2, NM, C), F32),
            shape((NM, N, HD), F32),
            shape((2, S, C), F32),
            shape((2, S, N, HD), F32),
        ),
        in_specs=[SMEM] * 3 + [ANY] * len(operands),
        out_specs=(ANY,) * 9,
        scratch_shapes=[vm((4, NR, C))]
        + [like(v) for v in operands[1:]]
        + [
            vm((2, S, QW + 2 * W)),
            vm((2, S, A, HD), BF16),
            vm((L, 16, C // 4), BF16),
            vm((R - 1, N, C), BF16),
            vm((R - 1, 16, C // 4), BF16),
            vm((R - 1, 16, C // 4), BF16),
            vm((R - 1, A, HD), BF16),
            vm((R - 1, A, HD), BF16),
            vm((2, S, AH, HD), BF16),
            vm((S, AH, HD), BF16),
            vm((R - 1, AH, HD), BF16),
            vm((R - 1, AH, HD), BF16),
            vm((4, S, C)),
            vm((NR, C)),
            vm((NR, C)),
            vm((NR, N, HD)),
            vm((NR, N, HD)),
            vm((S, C)),
            vm((S, C)),
            vm((S, N, HD)),
            vm((S, N, HD)),
            vm((N, C)),
            vm((S, C)),
            vm((S, C), BF16),
            vm((T, NR, rank + HD)),
            vm((T, S, rank + HD)),
            dma((len(operands) + 2,)),
            dma((11,)),
        ]
        + [dma((R - 1,))] * 8
        + [dma((2, T))] * 2,
        compiler_params=pltpu.CompilerParams(
            collective_id=0, has_side_effects=True, vmem_limit_bytes=58 * 1024 * 1024
        ),
        name="exchange",
    )(turned, lengths, page_table.T, *operands)
    whole = lambda v: pl.BlockSpec(v.shape, lambda g, m, i: (0,) * v.ndim)
    rest = rest + [a_log, row(skip_d), mamba_z, m_one]
    here = jnp.full((1,), lax.axis_index("replica"), jnp.int32)
    final_ssm, mamba_out = pl.pallas_call(
        functools.partial(finish_kernel, (R, S, L)),
        grid_spec=pltpu.PrefetchScalarGridSpec(
            num_scalar_prefetch=2,
            grid=(S,),
            in_specs=[
                pl.BlockSpec((1, N, C), lambda g, m, i: (g, 0, 0)),
                pl.BlockSpec((1, N, C), lambda g, m, i: (arrival(m, i[0], g, R, S, L)[1], 0, 0)),
            ]
            + [whole(v) for v in rest],
            out_specs=[
                pl.BlockSpec((1, N, C), lambda g, m, i: (g, 0, 0)),
                pl.BlockSpec((2, S, C), lambda g, m, i: (0, 0, 0)),
            ],
            scratch_shapes=[pltpu.VMEM((N, C), F32), pltpu.VMEM((S, C), F32)],
        ),
        out_shape=(shape((S, N, C), F32), shape((2, S, C), BF16)),
        compiler_params=pltpu.CompilerParams(vmem_limit_bytes=58 * 1024 * 1024),
        name="finish",
    )(turned, here, state_one, got_state, *rest)
    return (
        att[:, :, :H].reshape(2, S, QW),
        mamba_out,
        final_ssm,
        jnp.transpose(fconv, (1, 0, 2)),
    )


def solution(mesh):
    row, both = P("replica", None, "tensor"), P(None, "replica", "tensor")
    in_specs = (
        P(),
        P("replica", None),
        row,
        row,
        both,
        both,
        both,
        row,
        row,
        both,
        both,
        P(None, "tensor"),
        P("tensor"),
        P("tensor", None),
        P("tensor", None),
        P(None, "tensor"),
        P("tensor"),
        P(None, "tensor"),
        P("tensor"),
        P(),
    )
    return jax.shard_map(
        shards, mesh=mesh, in_specs=in_specs, out_specs=(both, both, row, row), check_vma=False
    )
```

```python
import functools
import math

import jax
import jax.numpy as jnp
from jax import lax
from jax.experimental import pallas as pl
from jax.experimental.pallas import tpu as pltpu
from jax.sharding import PartitionSpec as P

HD = 128
F32, BF16 = jnp.float32, jnp.bfloat16
MESH = pl.DeviceIdType.MESH
ANY = pl.BlockSpec(memory_space=pl.ANY)
SMEM = pl.BlockSpec(memory_space=pltpu.SMEM)


def round_up(n, m):
    return (n + m - 1) // m * m


def silu(v):
    return v / (1.0 + jnp.exp(-v))


def softplus(v):
    return jnp.maximum(v, 0.0) + jnp.log1p(jnp.exp(-jnp.abs(v)))


def chunks(total, most=512):
    step = min(most, total)
    return [slice(i, i + step) for i in range(0, total, step)]


def exchange_kernel(
    sizes,
    moves,
    lengths,
    pages,
    conv_hbm,
    mx_hbm,
    q_hbm,
    nk_hbm,
    nv_hbm,
    states_hbm,
    keys_hbm,
    vals_hbm,
    conv_w_hbm,
    conv_b_hbm,
    down_hbm,
    bc_hbm,
    up_hbm,
    dt_b_hbm,
    a_log_hbm,
    skip_hbm,
    mz_hbm,
    stay_out,
    got_state,
    att_out,
    fconv,
    m_one,
    vec_moved,
    b_moved,
    vec_two,
    bc_two,
    y_out,
    win,
    mx,
    queries,
    nk,
    nv,
    h,
    keys,
    vals,
    conv_w,
    conv_b,
    down,
    bc_w,
    up,
    dt_b,
    a_log,
    skip,
    mz,
    flat,
    asks,
    pack,
    send_state,
    send_small,
    got_small,
    send_ask,
    got_ask,
    att_two,
    send_att,
    got_att,
    win_two,
    xc_all,
    dt_all,
    b_all,
    c_all,
    xc_two,
    dt_two,
    b_two,
    c_two,
    rate,
    y,
    y_stay,
    stay,
    att_flat,
    att_bf,
    m_buf,
    part,
    part_two,
    load_sem,
    save_sem,
    state_s,
    state_r,
    small_s,
    small_r,
    ask_s,
    ask_r,
    att_s,
    att_r,
    part_s,
    part_r,
):
    R, T, S, L, H, KV = sizes
    C = h.shape[2]
    N = a_log.shape[0]
    NR = win.shape[1]
    rank = down.shape[1]
    page = keys.shape[1]
    n_pages = pages.shape[0]
    QW, W = queries.shape[2], keys.shape[2]
    A = asks.shape[2]
    me = lax.axis_index("replica")
    core = lax.axis_index("tensor")

    pairs = [(conv_hbm.at[k], win.at[k, pl.ds(0, S)]) for k in range(3)] + [
        (mx_hbm, mx),
        (q_hbm, queries),
        (nk_hbm, nk),
        (nv_hbm, nv),
        (states_hbm, h),
        (keys_hbm, keys),
        (vals_hbm, vals),
        (conv_w_hbm, conv_w),
        (conv_b_hbm, conv_b),
        (down_hbm, down),
        (bc_hbm, bc_w),
        (up_hbm, up),
        (dt_b_hbm, dt_b),
        (a_log_hbm, a_log),
        (skip_hbm, skip),
        (mz_hbm, mz),
    ]
    loads = [
        pltpu.make_async_copy(src, dst, load_sem.at[i]) for i, (src, dst) in enumerate(pairs)
    ]
    for load in loads:
        load.start()
    saves = []

    def save(src, dst):
        copy = pltpu.make_async_copy(src, dst, save_sem.at[len(saves)])
        copy.start()
        saves.append(copy)

    barrier = pltpu.get_barrier_semaphore()

    def greet(k, _):
        pl.semaphore_signal(
            barrier, inc=1, device_id={"replica": lax.rem(me + k, R)}, device_id_type=MESH
        )
        return 0

    def greet_core(k, _):
        pl.semaphore_signal(
            barrier, inc=1, device_id={"tensor": lax.rem(core + k, T)}, device_id_type=MESH
        )
        return 0

    lax.fori_loop(1, R, greet, 0)
    lax.fori_loop(1, T, greet_core, 0)

    shift = [lax.div(moves[1, j], S) for j in range(L)]
    out_slot = [lax.rem(moves[0, me * L + j], S) for j in range(L)]
    lane_of = [jnp.maximum(shift[j] - 1, 0) for j in range(L)]
    in_slot = [
        lax.rem(moves[1, lax.rem(me - shift[j] + R, R) * L + j], S) for j in range(L)
    ]

    def pick(values, k):
        found = values[0]
        for j in range(1, L):
            found = jnp.where(shift[j] == k, values[j], found)
        return found

    def source(g):
        row, lane = g, 0
        for j in range(L):
            hit = in_slot[j] == g
            row = jnp.where(hit, S + j, row)
            lane = jnp.where(hit, lane_of[j], lane)
        return row, lane

    def lane_copy(src, dst, send, recv, k, forward=True):
        to = lax.rem(me + k, R) if forward else lax.rem(me - k + R, R)
        return pltpu.make_async_remote_copy(
            src_ref=src.at[k - 1],
            dst_ref=dst.at[k - 1],
            send_sem=send.at[k - 1],
            recv_sem=recv.at[k - 1],
            device_id={"replica": to},
            device_id_type=MESH,
        )

    ask_copy = lambda k: lane_copy(send_ask, got_ask, ask_s, ask_r, k, False)
    small_copy = lambda k: lane_copy(send_small, got_small, small_s, small_r, k)
    state_copy = lambda k: lane_copy(send_state, got_state, state_s, state_r, k)
    att_copy = lambda k: lane_copy(send_att, got_att, att_s, att_r, k)

    for load in loads[4:7]:
        load.wait()
    for t in range(2):
        flat[t, :, :QW] = queries[t].astype(F32)
        flat[t, :, QW : QW + W] = nk[t].astype(F32)
        flat[t, :, QW + W :] = nv[t].astype(F32)

    def tile_up(g, _):
        for t in range(2):
            line = flat[t, pl.ds(g, 1), :]
            parts = [line[:, i * HD : (i + 1) * HD] for i in range(H + 2 * KV)]
            if A > H + 2 * KV:
                parts.append(jnp.zeros((A - H - 2 * KV, HD), F32))
            asks[t, g] = jnp.concatenate(parts, axis=0).astype(BF16)
        return 0

    lax.fori_loop(0, S, tile_up, 0)

    for load in loads[:4]:
        load.wait()
    win[3, :S] = mx[0].astype(F32)
    for j in range(L):
        lines = [win[k, pl.ds(out_slot[j], 1), :] for k in range(4)]
        pack[j] = jnp.concatenate(
            [line[:, i * (C // 4) : (i + 1) * (C // 4)] for line in lines for i in range(4)],
            axis=0,
        ).astype(BF16)

    pl.semaphore_wait(barrier, R - 1 + T - 1)

    def send_first(k, _):
        send_ask[k - 1] = asks[1, pick(in_slot, k)]
        ask_copy(k).start()
        send_small[k - 1] = pack[pick(range(L), k)]
        small_copy(k).start()
        return 0

    lax.fori_loop(1, R, send_first, 0)
    loads[7].wait()

    def send_states(k, _):
        slot = pick(out_slot, k)
        for c in chunks(C):
            send_state[k - 1, :, c] = h[slot, :, c].astype(BF16)
        state_copy(k).start()
        return 0

    lax.fori_loop(1, R, send_states, 0)

    loads[8].wait()
    loads[9].wait()
    lax.fori_loop(1, R, lambda k, _: (ask_copy(k).wait(), 0)[1], 0)

    rows = 2 * H
    head_of = lax.broadcasted_iota(jnp.int32, (rows, 1), 0) % H // (H // KV)
    step_of = lax.broadcasted_iota(jnp.int32, (rows, 1), 0) // H
    ask_col = lax.broadcasted_iota(jnp.int32, (rows, asks.shape[2]), 1)
    pos = lax.broadcasted_iota(jnp.int32, (rows, n_pages * page), 1)
    is_key = ask_col == H + head_of
    is_val = ask_col == H + KV + head_of
    nt = (((1,), (1,)), ((), ()))
    nn = (((1,), (0,)), ((), ()))

    def line_up(tile):
        return jnp.concatenate([tile[i : i + 1] for i in range(H)], axis=1)

    def attend(g):
        length = lengths[me * S + g]
        gone = jnp.int32(0)
        lane = jnp.int32(0)
        for j in range(L):
            hit = out_slot[j] == g
            gone = jnp.where(hit, 1, gone)
            lane = jnp.where(hit, lane_of[j], lane)
        one = asks[0, g]
        two = jnp.where(gone == 1, got_ask[lane].astype(F32), asks[1, g].astype(F32)).astype(BF16)
        q = jnp.concatenate([one.astype(F32)[:H], two.astype(F32)[:H]], axis=0)
        qb = q.astype(BF16)
        wide = jnp.concatenate(
            [jnp.where(head_of == i, q, 0.0) for i in range(KV)], axis=1
        ).astype(BF16)
        scores = jnp.concatenate(
            [
                lax.dot_general(wide, keys[pages[p, g]], nt, preferred_element_type=F32)
                for p in range(n_pages)
            ],
            axis=1,
        )
        new_one = lax.dot_general(qb, one, nt, preferred_element_type=F32)
        new_two = lax.dot_general(qb, two, nt, preferred_element_type=F32)
        new_one = jnp.sum(jnp.where(is_key, new_one, 0.0), axis=1, keepdims=True)
        new_two = jnp.sum(jnp.where(is_key, new_two, 0.0), axis=1, keepdims=True)
        at_one, at_two = pos == length, pos == length + 1
        scores = jnp.where(at_one, new_one, jnp.where(at_two, new_two, scores))
        scores = scores * (1.0 / math.sqrt(HD))
        scores = jnp.where(pos <= length + step_of, scores, -1e30)
        expo = jnp.exp(scores - jnp.max(scores, axis=1, keepdims=True))
        w = expo / jnp.sum(expo, axis=1, keepdims=True)
        w_one = jnp.sum(jnp.where(at_one, w, 0.0), axis=1, keepdims=True)
        w_two = jnp.sum(jnp.where(at_two, w, 0.0), axis=1, keepdims=True)
        w = jnp.where(at_one | at_two, 0.0, w).astype(BF16)
        mixed = lax.dot_general(
            w[:, :page], vals[pages[0, g]], nn, preferred_element_type=F32
        )
        for p in range(1, n_pages):
            mixed += lax.dot_general(
                w[:, p * page : (p + 1) * page],
                vals[pages[p, g]],
                nn,
                preferred_element_type=F32,
            )
        out = lax.dot_general(
            jnp.where(is_val, w_one, 0.0).astype(BF16), one, nn, preferred_element_type=F32
        ) + lax.dot_general(
            jnp.where(is_val, w_two, 0.0).astype(BF16), two, nn, preferred_element_type=F32
        )
        for i in range(KV):
            out += jnp.where(head_of == i, mixed[:, i * HD : (i + 1) * HD], 0.0)
        first, second = out[:H], out[H:]
        if att_two.shape[1] > H:
            pad = jnp.zeros((att_two.shape[1] - H, HD), F32)
            first = jnp.concatenate([first, pad], axis=0)
            second = jnp.concatenate([second, pad], axis=0)
        return first.astype(BF16), second.astype(BF16)

    batch = 4 if S % 4 == 0 else 1

    def attend_some(i, _):
        results = [attend(i * batch + b) for b in range(batch)]
        for b, (first, second) in enumerate(results):
            att_flat[0, pl.ds(i * batch + b, 1), :] = line_up(first.astype(F32))
            att_two[i * batch + b] = second
        return 0

    lax.fori_loop(0, S // batch, attend_some, 0)

    def send_back(k, _):
        send_att[k - 1] = att_two[pick(out_slot, k)]
        att_copy(k).start()
        return 0

    lax.fori_loop(1, R, send_back, 0)

    lax.fori_loop(1, R, lambda k, _: (small_copy(k).wait(), 0)[1], 0)
    for j in range(L):
        tile = got_small[lane_of[j]].astype(F32)
        for k in range(4):
            win[k, S + j : S + j + 1] = jnp.concatenate(
                [tile[4 * k + i : 4 * k + i + 1] for i in range(4)], axis=1
            )
    for k in range(4):
        win[k, S + L :] = jnp.zeros((NR - S - L, C), F32)

    def project(src, n, xc_ref, buf):
        low = jnp.zeros((n, rank), F32)
        bc = jnp.zeros((n, bc_w.shape[0]), F32)
        for c in chunks(C):
            total = conv_b[:, c] + src(0, c) * conv_w[0:1, c]
            for k in range(1, 4):
                total += src(k, c) * conv_w[k : k + 1, c]
            xb = silu(total).astype(BF16)
            xc_ref[:, c] = xb.astype(F32)
            low += lax.dot_general(xb, down[c], nn, preferred_element_type=F32)
            bc += lax.dot_general(xb, bc_w[:, c], nt, preferred_element_type=F32)
        buf[core, :, :rank] = low
        buf[core, :, rank:] = jnp.concatenate(
            [bc, jnp.zeros((n, HD - bc.shape[1]), F32)], axis=1
        )

    def core_copy(buf, which, k):
        return pltpu.make_async_remote_copy(
            src_ref=buf.at[core],
            dst_ref=buf.at[core],
            send_sem=part_s.at[which, k],
            recv_sem=part_r.at[which, k],
            device_id={"tensor": lax.rem(core + k, T)},
            device_id_type=MESH,
        )

    def reduce_parts(buf, which):
        lax.fori_loop(1, T, lambda k, _: (core_copy(buf, which, k).start(), 0)[1], 0)
        lax.fori_loop(1, T, lambda k, _: (core_copy(buf, which, k).wait(), 0)[1], 0)
        total = buf[0]
        for t in range(1, T):
            total += buf[t]
        return total

    def steps(total, n, dt_ref, b_ref, c_ref):
        low = total[:, :rank].astype(BF16)
        for c in chunks(C):
            dt_ref[:, c] = softplus(
                lax.dot_general(low, up[:, c], nn, preferred_element_type=F32) + dt_b[:, c]
            )
        turned = total[:, rank : rank + HD].T
        for i in range(n):
            b_ref[i] = jnp.broadcast_to(turned[:N, i : i + 1], (N, HD))
            c_ref[i] = jnp.broadcast_to(turned[N : 2 * N, i : i + 1], (N, HD))

    for load in loads[10:]:
        load.wait()
    rate[...] = jnp.exp(a_log[...])
    project(lambda k, c: win[k, :, c], NR, xc_all, part)
    steps(reduce_parts(part, 0), NR, dt_all, b_all, c_all)
    moved = pl.ds(S, NR - S)
    save(dt_all.at[moved], vec_moved.at[0])
    save(xc_all.at[moved], vec_moved.at[1])
    save(b_all.at[moved], b_moved)

    for g in range(S):
        row, _ = source(g)
        for k in range(3):
            win_two[k, g : g + 1] = win[k + 1, pl.ds(row, 1), :]
    win_two[3] = mx[1].astype(F32)
    save(win_two.at[pl.ds(1, 3)], fconv)
    project(lambda k, c: win_two[k, :, c], S, xc_two, part_two)
    steps(reduce_parts(part_two, 1), S, dt_two, b_two, c_two)
    save(dt_two, vec_two.at[0])
    save(xc_two, vec_two.at[1])
    save(b_two, bc_two.at[0])
    save(c_two, bc_two.at[1])

    def scan(g, _):
        for c in chunks(C, 2048):
            reps = (c.stop - c.start) // HD
            dt = dt_all[pl.ds(g, 1), c]
            x = xc_all[pl.ds(g, 1), c]
            new = jnp.exp(-dt * rate[:, c]) * h[g, :, c]
            new += jnp.concatenate([b_all[g]] * reps, axis=1) * (dt * x)
            line = jnp.sum(jnp.concatenate([c_all[g]] * reps, axis=1) * new, axis=0, keepdims=True)
            h[g, :, c] = new
            y[pl.ds(g, 1), c] = line
        return 0

    lax.fori_loop(0, S, scan, 0)

    stay_slots = staying(out_slot, S, S - L)

    def scan_stay(i, _):
        g = stay_slots[0]
        for n in range(1, S - L):
            g = jnp.where(i == n, stay_slots[n], g)
        for c in chunks(C, 2048):
            reps = (c.stop - c.start) // HD
            dt = dt_two[pl.ds(g, 1), c]
            x = xc_two[pl.ds(g, 1), c]
            new = jnp.exp(-dt * rate[:, c]) * h[g, :, c]
            new += jnp.concatenate([b_two[g]] * reps, axis=1) * (dt * x)
            line = jnp.sum(jnp.concatenate([c_two[g]] * reps, axis=1) * new, axis=0, keepdims=True)
            stay[i, :, c] = new
            y_stay[pl.ds(i, 1), c] = line
        return 0

    lax.fori_loop(0, S - L, scan_stay, 0)
    save(stay, stay_out)
    save(y_stay, y_out)
    for c in chunks(C):
        m_buf[:, c] = (
            (y[:, c] + skip[:, c] * xc_all[:S, c]) * silu(mz[0, :, c].astype(F32))
        ).astype(BF16)

    save(m_buf, m_one)

    lax.fori_loop(1, R, lambda k, _: (att_copy(k).wait(), 0)[1], 0)
    for g in range(S):
        row, lane = source(g)
        tile = jnp.where(row >= S, got_att[lane].astype(F32), att_two[g].astype(F32))
        att_flat[1, g : g + 1] = line_up(tile)
    att_bf[...] = att_flat[...].astype(BF16)
    save(att_bf, att_out)
    for copy in saves:
        copy.wait()
    lax.fori_loop(1, R, lambda k, _: (state_copy(k).wait(), 0)[1], 0)


def finish_kernel(
    sizes,
    moves,
    stay,
    got_state,
    att_in,
    fconv_in,
    m_one,
    vec_moved_hbm,
    b_moved_hbm,
    vec_two_hbm,
    bc_two_hbm,
    y_hbm,
    a_log_hbm,
    skip_hbm,
    mz_hbm,
    att,
    out,
    final,
    fconv,
    arrived,
    done,
    vec_moved,
    b_moved,
    vec_two,
    bc_two,
    y_stay,
    rate,
    skip,
    mz,
    y,
    m_two,
    load_sem,
    arrive_sem,
    stay_sem,
    done_sem,
    pass_sem,
):
    R, S, L = sizes
    C = final.shape[2]
    me = lax.axis_index("replica")
    shift = [lax.div(moves[1, j], S) for j in range(L)]
    slot = [lax.rem(moves[1, lax.rem(me - shift[j] + R, R) * L + j], S) for j in range(L)]
    pairs = [
        (a_log_hbm, rate),
        (vec_moved_hbm, vec_moved),
        (b_moved_hbm, b_moved),
        (vec_two_hbm, vec_two),
        (bc_two_hbm, bc_two),
        (y_hbm, y_stay),
        (skip_hbm, skip),
        (mz_hbm, mz),
    ]
    loads = [
        pltpu.make_async_copy(src, dst, load_sem.at[i]) for i, (src, dst) in enumerate(pairs)
    ]
    arrivals = [
        pltpu.make_async_copy(
            got_state.at[jnp.maximum(shift[j] - 1, 0)], arrived.at[j], arrive_sem.at[j]
        )
        for j in range(L)
    ]
    for load in loads[:5]:
        load.start()
    for copy in arrivals:
        copy.start()
    for load in loads[5:]:
        load.start()
    stay_slots = staying(slot, S, S - L)
    passes = [
        pltpu.make_async_copy(stay.at[i], final.at[stay_slots[i]], stay_sem.at[i])
        for i in range(S - L)
    ] + [
        pltpu.make_async_copy(att_in, att, pass_sem.at[0]),
        pltpu.make_async_copy(fconv_in, fconv, pass_sem.at[1]),
        pltpu.make_async_copy(m_one, out.at[0], pass_sem.at[2]),
    ]
    for copy in passes:
        copy.start()
    wide = lambda v, c: jnp.concatenate([v] * ((c.stop - c.start) // HD), axis=1)
    for load in loads:
        load.wait()
    rate[...] = jnp.exp(rate[...])
    for i in range(S - L):
        y[pl.ds(stay_slots[i], 1), :] = y_stay[i : i + 1]
    results = []
    for j in range(L):
        g = slot[j]
        arrivals[j].wait()
        for c in chunks(C, 1024):
            dt, x = vec_moved[0, j : j + 1, c], vec_moved[1, j : j + 1, c]
            new = jnp.exp(-dt * rate[:, c]) * arrived[j, :, c].astype(F32)
            new += wide(b_moved[j], c) * (dt * x)
            dt, x = vec_two[0, pl.ds(g, 1), c], vec_two[1, pl.ds(g, 1), c]
            new = jnp.exp(-dt * rate[:, c]) * new + wide(bc_two[0, g], c) * (dt * x)
            line = jnp.sum(wide(bc_two[1, g], c) * new, axis=0, keepdims=True)
            done[j, :, c] = new
            y[pl.ds(g, 1), c] = line
        copy = pltpu.make_async_copy(done.at[j], final.at[g], done_sem.at[j])
        copy.start()
        results.append(copy)
    for c in chunks(C):
        m_two[:, c] = (
            (y[:, c] + skip[:, c] * vec_two[1, :, c]) * silu(mz[1, :, c].astype(F32))
        ).astype(BF16)
    last = pltpu.make_async_copy(m_two, out.at[1], pass_sem.at[3])
    last.start()
    for copy in passes + results + [last]:
        copy.wait()


def staying(moved, slots, count):
    found = [jnp.int32(0)] * count
    seen = jnp.int32(0)
    for g in range(slots):
        gone = moved[0] == g
        for slot in moved[1:]:
            gone = gone | (slot == g)
        for i in range(count):
            found[i] = jnp.where(~gone & (seen == i), g, found[i])
        seen = seen + jnp.where(gone, 0, 1)
    return found


def shards(
    lengths,
    page_table,
    key_pool,
    value_pool,
    queries,
    new_keys,
    new_values,
    conv_state,
    ssm_state,
    mamba_x,
    mamba_z,
    conv_weight,
    conv_bias,
    dt_down,
    bc_proj,
    dt_up,
    dt_bias,
    a_log,
    skip_d,
    moves,
):
    R, T = lax.axis_size("replica"), lax.axis_size("tensor")
    S, N, C = ssm_state.shape
    L = moves.shape[0] // R
    QW, W = queries.shape[2], key_pool.shape[2]
    H, KV = QW // HD, W // HD
    A = round_up(H + 2 * KV, 16)
    AH = round_up(H, 16)
    NR = S + round_up(L, 16)
    rank = dt_down.shape[1]

    row = lambda v: v.reshape(1, C)
    shape = jax.ShapeDtypeStruct
    dma = pltpu.SemaphoreType.DMA
    vm = lambda dims, kind=F32: pltpu.VMEM(dims, kind)
    like = lambda v: pltpu.VMEM(v.shape, v.dtype)
    NM = NR - S
    turned = moves.T
    operands = (
        jnp.transpose(conv_state, (1, 0, 2)),
        mamba_x,
        queries,
        new_keys,
        new_values,
        ssm_state,
        key_pool,
        value_pool,
        conv_weight,
        row(conv_bias),
        dt_down,
        bc_proj.T,
        dt_up,
        row(dt_bias),
        a_log,
        row(skip_d),
        mamba_z,
    )
    results = pl.pallas_call(
        functools.partial(exchange_kernel, (R, T, S, L, H, KV)),
        out_shape=(
            shape((S - L, N, C), F32),
            shape((R - 1, N, C), BF16),
            shape((2, S, QW), BF16),
            shape((3, S, C), F32),
            shape((S, C), BF16),
            shape((2, NM, C), F32),
            shape((NM, N, HD), F32),
            shape((2, S, C), F32),
            shape((2, S, N, HD), F32),
            shape((S - L, C), F32),
        ),
        in_specs=[SMEM] * 3 + [ANY] * len(operands),
        out_specs=(ANY,) * 10,
        scratch_shapes=[vm((4, NR, C))]
        + [like(v) for v in operands[1:]]
        + [
            vm((2, S, QW + 2 * W)),
            vm((2, S, A, HD), BF16),
            vm((L, 16, C // 4), BF16),
            vm((R - 1, N, C), BF16),
            vm((R - 1, 16, C // 4), BF16),
            vm((R - 1, 16, C // 4), BF16),
            vm((R - 1, A, HD), BF16),
            vm((R - 1, A, HD), BF16),
            vm((S, AH, HD), BF16),
            vm((R - 1, AH, HD), BF16),
            vm((R - 1, AH, HD), BF16),
            vm((4, S, C)),
            vm((NR, C)),
            vm((NR, C)),
            vm((NR, N, HD)),
            vm((NR, N, HD)),
            vm((S, C)),
            vm((S, C)),
            vm((S, N, HD)),
            vm((S, N, HD)),
            vm((N, C)),
            vm((S, C)),
            vm((S - L, C)),
            vm((S - L, N, C)),
            vm((2, S, QW)),
            vm((2, S, QW), BF16),
            vm((S, C), BF16),
            vm((T, NR, rank + HD)),
            vm((T, S, rank + HD)),
            dma((len(operands) + 2,)),
            dma((12,)),
        ]
        + [dma((R - 1,))] * 8
        + [dma((2, T))] * 2,
        compiler_params=pltpu.CompilerParams(
            collective_id=0, has_side_effects=True, vmem_limit_bytes=58 * 1024 * 1024
        ),
        name="exchange",
    )(turned, lengths, page_table.T, *operands)
    att, mamba_out, final_ssm, fconv = pl.pallas_call(
        functools.partial(finish_kernel, (R, S, L)),
        in_specs=[SMEM] + [ANY] * 13,
        out_specs=[ANY] * 4,
        out_shape=(
            shape((2, S, QW), BF16),
            shape((2, S, C), BF16),
            shape((S, N, C), F32),
            shape((3, S, C), F32),
        ),
        scratch_shapes=[
            vm((L, N, C), BF16),
            vm((L, N, C)),
            vm((2, NM, C)),
            vm((NM, N, HD)),
            vm((2, S, C)),
            vm((2, S, N, HD)),
            vm((S - L, C)),
            vm((N, C)),
            vm((1, C)),
            vm((2, S, C), BF16),
            vm((S, C)),
            vm((S, C), BF16),
            dma((8,)),
            dma((L,)),
            dma((S - L,)),
            dma((L,)),
            dma((4,)),
        ],
        compiler_params=pltpu.CompilerParams(vmem_limit_bytes=58 * 1024 * 1024),
        name="finish",
    )(turned, *results, a_log, row(skip_d), mamba_z)
    return att, mamba_out, final_ssm, jnp.transpose(fconv, (1, 0, 2))


def solution(mesh):
    row, both = P("replica", None, "tensor"), P(None, "replica", "tensor")
    in_specs = (
        P(),
        P("replica", None),
        row,
        row,
        both,
        both,
        both,
        row,
        row,
        both,
        both,
        P(None, "tensor"),
        P("tensor"),
        P("tensor", None),
        P("tensor", None),
        P(None, "tensor"),
        P("tensor"),
        P(None, "tensor"),
        P("tensor"),
        P(),
    )
    return jax.shard_map(
        shards, mesh=mesh, in_specs=in_specs, out_specs=(both, both, row, row), check_vma=False
    )
```

```python
import functools
import math

import jax
import jax.numpy as jnp
from jax import lax
from jax.experimental import pallas as pl
from jax.experimental.pallas import tpu as pltpu
from jax.sharding import PartitionSpec as P

HD = 128
F32, BF16 = jnp.float32, jnp.bfloat16
MESH = pl.DeviceIdType.MESH
ANY = pl.BlockSpec(memory_space=pl.ANY)
SMEM = pl.BlockSpec(memory_space=pltpu.SMEM)


def round_up(n, m):
    return (n + m - 1) // m * m


def silu(v):
    return v / (1.0 + jnp.exp(-v))


def softplus(v):
    return jnp.maximum(v, 0.0) + jnp.log1p(jnp.exp(-jnp.abs(v)))


def chunks(total, most=512):
    step = min(most, total)
    return [slice(i, i + step) for i in range(0, total, step)]


def exchange_kernel(
    sizes,
    moves,
    lengths,
    pages,
    conv_hbm,
    mx_hbm,
    q_hbm,
    nk_hbm,
    nv_hbm,
    states_hbm,
    keys_hbm,
    vals_hbm,
    conv_w_hbm,
    conv_b_hbm,
    down_hbm,
    bc_hbm,
    up_hbm,
    dt_b_hbm,
    a_log_hbm,
    skip_hbm,
    mz_hbm,
    stay_out,
    got_state,
    att_out,
    fconv,
    m_one,
    vec_moved,
    b_moved,
    vec_two,
    bc_two,
    y_out,
    win,
    mx,
    queries,
    nk,
    nv,
    h,
    keys,
    vals,
    conv_w,
    conv_b,
    down,
    bc_w,
    up,
    dt_b,
    a_log,
    skip,
    mz,
    flat,
    asks,
    pack,
    send_state,
    send_small,
    got_small,
    send_ask,
    got_ask,
    att_two,
    send_att,
    got_att,
    win_two,
    xc_all,
    dt_all,
    b_all,
    c_all,
    xc_two,
    dt_two,
    b_two,
    c_two,
    rate,
    y,
    y_stay,
    stay,
    att_flat,
    att_bf,
    m_buf,
    part,
    part_two,
    load_sem,
    save_sem,
    state_s,
    state_r,
    small_s,
    small_r,
    ask_s,
    ask_r,
    att_s,
    att_r,
    part_s,
    part_r,
):
    R, T, S, L, H, KV = sizes
    C = h.shape[2]
    N = a_log.shape[0]
    NR = win.shape[1]
    rank = down.shape[1]
    page = keys.shape[1]
    n_pages = pages.shape[0]
    QW, W = queries.shape[2], keys.shape[2]
    A = asks.shape[2]
    me = lax.axis_index("replica")
    core = lax.axis_index("tensor")

    pairs = [(conv_hbm.at[k], win.at[k, pl.ds(0, S)]) for k in range(3)] + [
        (mx_hbm, mx),
        (q_hbm, queries),
        (nk_hbm, nk),
        (nv_hbm, nv),
        (states_hbm, h),
        (keys_hbm, keys),
        (vals_hbm, vals),
        (conv_w_hbm, conv_w),
        (conv_b_hbm, conv_b),
        (down_hbm, down),
        (bc_hbm, bc_w),
        (up_hbm, up),
        (dt_b_hbm, dt_b),
        (a_log_hbm, a_log),
        (skip_hbm, skip),
        (mz_hbm, mz),
    ]
    loads = [
        pltpu.make_async_copy(src, dst, load_sem.at[i]) for i, (src, dst) in enumerate(pairs)
    ]
    loads[7].start()
    for load in loads[:7] + loads[8:]:
        load.start()
    saves = []

    def save(src, dst):
        copy = pltpu.make_async_copy(src, dst, save_sem.at[len(saves)])
        copy.start()
        saves.append(copy)

    barrier = pltpu.get_barrier_semaphore()

    def greet(k, _):
        pl.semaphore_signal(
            barrier, inc=1, device_id={"replica": lax.rem(me + k, R)}, device_id_type=MESH
        )
        return 0

    def greet_core(k, _):
        pl.semaphore_signal(
            barrier, inc=1, device_id={"tensor": lax.rem(core + k, T)}, device_id_type=MESH
        )
        return 0

    lax.fori_loop(1, R, greet, 0)
    lax.fori_loop(1, T, greet_core, 0)

    shift = [lax.div(moves[1, j], S) for j in range(L)]
    out_slot = [lax.rem(moves[0, me * L + j], S) for j in range(L)]
    lane_of = [jnp.maximum(shift[j] - 1, 0) for j in range(L)]
    in_slot = [
        lax.rem(moves[1, lax.rem(me - shift[j] + R, R) * L + j], S) for j in range(L)
    ]

    def pick(values, k):
        found = values[0]
        for j in range(1, L):
            found = jnp.where(shift[j] == k, values[j], found)
        return found

    def source(g):
        row, lane = g, 0
        for j in range(L):
            hit = in_slot[j] == g
            row = jnp.where(hit, S + j, row)
            lane = jnp.where(hit, lane_of[j], lane)
        return row, lane

    def lane_copy(src, dst, send, recv, k, forward=True):
        to = lax.rem(me + k, R) if forward else lax.rem(me - k + R, R)
        return pltpu.make_async_remote_copy(
            src_ref=src.at[k - 1],
            dst_ref=dst.at[k - 1],
            send_sem=send.at[k - 1],
            recv_sem=recv.at[k - 1],
            device_id={"replica": to},
            device_id_type=MESH,
        )

    ask_copy = lambda k: lane_copy(send_ask, got_ask, ask_s, ask_r, k, False)
    small_copy = lambda k: lane_copy(send_small, got_small, small_s, small_r, k)
    state_copy = lambda k: lane_copy(send_state, got_state, state_s, state_r, k)
    att_copy = lambda k: lane_copy(send_att, got_att, att_s, att_r, k)

    pl.semaphore_wait(barrier, R - 1 + T - 1)

    def lane(i):
        return 1 + lax.rem(7 * i, R - 1)

    def send_states(i, _):
        k = lane(i)
        slot = pick(out_slot, k)
        for c in chunks(C):
            send_state[k - 1, :, c] = h[slot, :, c].astype(BF16)
        state_copy(k).start()
        return 0

    def send_small_rows(i, _):
        k = lane(i)
        send_small[k - 1] = pack[pick(range(L), k)]
        small_copy(k).start()
        return 0

    def send_asks(i, _):
        k = lane(i)
        send_ask[k - 1] = asks[1, pick(in_slot, k)]
        ask_copy(k).start()
        return 0

    early = min(4, R - 1)
    loads[7].wait()
    lax.fori_loop(0, early, send_states, 0)

    for load in loads[4:7]:
        load.wait()
    for t in range(2):
        flat[t, :, :QW] = queries[t].astype(F32)
        flat[t, :, QW : QW + W] = nk[t].astype(F32)
        flat[t, :, QW + W :] = nv[t].astype(F32)

    def tile_up(g, _):
        for t in range(2):
            line = flat[t, pl.ds(g, 1), :]
            parts = [line[:, i * HD : (i + 1) * HD] for i in range(H + 2 * KV)]
            if A > H + 2 * KV:
                parts.append(jnp.zeros((A - H - 2 * KV, HD), F32))
            asks[t, g] = jnp.concatenate(parts, axis=0).astype(BF16)
        return 0

    lax.fori_loop(0, S, tile_up, 0)

    for load in loads[:4]:
        load.wait()
    win[3, :S] = mx[0].astype(F32)
    for j in range(L):
        lines = [win[k, pl.ds(out_slot[j], 1), :] for k in range(4)]
        pack[j] = jnp.concatenate(
            [line[:, i * (C // 4) : (i + 1) * (C // 4)] for line in lines for i in range(4)],
            axis=0,
        ).astype(BF16)

    lax.fori_loop(0, R - 1, send_asks, 0)
    lax.fori_loop(0, R - 1, send_small_rows, 0)
    lax.fori_loop(early, R - 1, send_states, 0)

    loads[8].wait()
    loads[9].wait()
    lax.fori_loop(1, R, lambda k, _: (ask_copy(k).wait(), 0)[1], 0)

    rows = 2 * H
    head_of = lax.broadcasted_iota(jnp.int32, (rows, 1), 0) % H // (H // KV)
    step_of = lax.broadcasted_iota(jnp.int32, (rows, 1), 0) // H
    ask_col = lax.broadcasted_iota(jnp.int32, (rows, asks.shape[2]), 1)
    pos = lax.broadcasted_iota(jnp.int32, (rows, n_pages * page), 1)
    is_key = ask_col == H + head_of
    is_val = ask_col == H + KV + head_of
    nt = (((1,), (1,)), ((), ()))
    nn = (((1,), (0,)), ((), ()))

    def line_up(tile):
        return jnp.concatenate([tile[i : i + 1] for i in range(H)], axis=1)

    def attend(g):
        length = lengths[me * S + g]
        gone = jnp.int32(0)
        lane = jnp.int32(0)
        for j in range(L):
            hit = out_slot[j] == g
            gone = jnp.where(hit, 1, gone)
            lane = jnp.where(hit, lane_of[j], lane)
        one = asks[0, g]
        two = jnp.where(gone == 1, got_ask[lane].astype(F32), asks[1, g].astype(F32)).astype(BF16)
        q = jnp.concatenate([one.astype(F32)[:H], two.astype(F32)[:H]], axis=0)
        qb = q.astype(BF16)
        wide = jnp.concatenate(
            [jnp.where(head_of == i, q, 0.0) for i in range(KV)], axis=1
        ).astype(BF16)
        scores = jnp.concatenate(
            [
                lax.dot_general(wide, keys[pages[p, g]], nt, preferred_element_type=F32)
                for p in range(n_pages)
            ],
            axis=1,
        )
        new_one = lax.dot_general(qb, one, nt, preferred_element_type=F32)
        new_two = lax.dot_general(qb, two, nt, preferred_element_type=F32)
        new_one = jnp.sum(jnp.where(is_key, new_one, 0.0), axis=1, keepdims=True)
        new_two = jnp.sum(jnp.where(is_key, new_two, 0.0), axis=1, keepdims=True)
        at_one, at_two = pos == length, pos == length + 1
        scores = jnp.where(at_one, new_one, jnp.where(at_two, new_two, scores))
        scores = scores * (1.0 / math.sqrt(HD))
        scores = jnp.where(pos <= length + step_of, scores, -1e30)
        expo = jnp.exp(scores - jnp.max(scores, axis=1, keepdims=True))
        w = expo / jnp.sum(expo, axis=1, keepdims=True)
        w_one = jnp.sum(jnp.where(at_one, w, 0.0), axis=1, keepdims=True)
        w_two = jnp.sum(jnp.where(at_two, w, 0.0), axis=1, keepdims=True)
        w = jnp.where(at_one | at_two, 0.0, w).astype(BF16)
        mixed = lax.dot_general(
            w[:, :page], vals[pages[0, g]], nn, preferred_element_type=F32
        )
        for p in range(1, n_pages):
            mixed += lax.dot_general(
                w[:, p * page : (p + 1) * page],
                vals[pages[p, g]],
                nn,
                preferred_element_type=F32,
            )
        out = lax.dot_general(
            jnp.where(is_val, w_one, 0.0).astype(BF16), one, nn, preferred_element_type=F32
        ) + lax.dot_general(
            jnp.where(is_val, w_two, 0.0).astype(BF16), two, nn, preferred_element_type=F32
        )
        for i in range(KV):
            out += jnp.where(head_of == i, mixed[:, i * HD : (i + 1) * HD], 0.0)
        first, second = out[:H], out[H:]
        if att_two.shape[1] > H:
            pad = jnp.zeros((att_two.shape[1] - H, HD), F32)
            first = jnp.concatenate([first, pad], axis=0)
            second = jnp.concatenate([second, pad], axis=0)
        return first.astype(BF16), second.astype(BF16)

    batch = 4 if S % 4 == 0 else 1

    def attend_some(i, _):
        results = [attend(i * batch + b) for b in range(batch)]
        for b, (first, second) in enumerate(results):
            att_flat[0, pl.ds(i * batch + b, 1), :] = line_up(first.astype(F32))
            att_two[i * batch + b] = second
        return 0

    lax.fori_loop(0, S // batch, attend_some, 0)

    def send_back(k, _):
        send_att[k - 1] = att_two[pick(out_slot, k)]
        att_copy(k).start()
        return 0

    lax.fori_loop(1, R, send_back, 0)

    lax.fori_loop(1, R, lambda k, _: (small_copy(k).wait(), 0)[1], 0)
    for j in range(L):
        tile = got_small[lane_of[j]].astype(F32)
        for k in range(4):
            win[k, S + j : S + j + 1] = jnp.concatenate(
                [tile[4 * k + i : 4 * k + i + 1] for i in range(4)], axis=1
            )
    for k in range(4):
        win[k, S + L :] = jnp.zeros((NR - S - L, C), F32)

    def project(src, n, xc_ref, buf):
        low = jnp.zeros((n, rank), F32)
        bc = jnp.zeros((n, bc_w.shape[0]), F32)
        for c in chunks(C):
            total = conv_b[:, c] + src(0, c) * conv_w[0:1, c]
            for k in range(1, 4):
                total += src(k, c) * conv_w[k : k + 1, c]
            xb = silu(total).astype(BF16)
            xc_ref[:, c] = xb.astype(F32)
            low += lax.dot_general(xb, down[c], nn, preferred_element_type=F32)
            bc += lax.dot_general(xb, bc_w[:, c], nt, preferred_element_type=F32)
        buf[core, :, :rank] = low
        buf[core, :, rank:] = jnp.concatenate(
            [bc, jnp.zeros((n, HD - bc.shape[1]), F32)], axis=1
        )

    def core_copy(buf, which, k):
        return pltpu.make_async_remote_copy(
            src_ref=buf.at[core],
            dst_ref=buf.at[core],
            send_sem=part_s.at[which, k],
            recv_sem=part_r.at[which, k],
            device_id={"tensor": lax.rem(core + k, T)},
            device_id_type=MESH,
        )

    def reduce_parts(buf, which):
        lax.fori_loop(1, T, lambda k, _: (core_copy(buf, which, k).start(), 0)[1], 0)
        lax.fori_loop(1, T, lambda k, _: (core_copy(buf, which, k).wait(), 0)[1], 0)
        total = buf[0]
        for t in range(1, T):
            total += buf[t]
        return total

    def steps(total, n, dt_ref, b_ref, c_ref):
        low = total[:, :rank].astype(BF16)
        for c in chunks(C):
            dt_ref[:, c] = softplus(
                lax.dot_general(low, up[:, c], nn, preferred_element_type=F32) + dt_b[:, c]
            )
        turned = total[:, rank : rank + HD].T
        for i in range(n):
            b_ref[i] = jnp.broadcast_to(turned[:N, i : i + 1], (N, HD))
            c_ref[i] = jnp.broadcast_to(turned[N : 2 * N, i : i + 1], (N, HD))

    for load in loads[10:]:
        load.wait()
    rate[...] = jnp.exp(a_log[...])
    project(lambda k, c: win[k, :, c], NR, xc_all, part)
    steps(reduce_parts(part, 0), NR, dt_all, b_all, c_all)
    moved = pl.ds(S, NR - S)
    save(dt_all.at[moved], vec_moved.at[0])
    save(xc_all.at[moved], vec_moved.at[1])
    save(b_all.at[moved], b_moved)

    for g in range(S):
        row, _ = source(g)
        for k in range(3):
            win_two[k, g : g + 1] = win[k + 1, pl.ds(row, 1), :]
    win_two[3] = mx[1].astype(F32)
    save(win_two.at[pl.ds(1, 3)], fconv)
    project(lambda k, c: win_two[k, :, c], S, xc_two, part_two)
    steps(reduce_parts(part_two, 1), S, dt_two, b_two, c_two)
    save(dt_two, vec_two.at[0])
    save(xc_two, vec_two.at[1])
    save(b_two, bc_two.at[0])
    save(c_two, bc_two.at[1])

    def scan(g, _):
        for c in chunks(C, 2048):
            reps = (c.stop - c.start) // HD
            dt = dt_all[pl.ds(g, 1), c]
            x = xc_all[pl.ds(g, 1), c]
            new = jnp.exp(-dt * rate[:, c]) * h[g, :, c]
            new += jnp.concatenate([b_all[g]] * reps, axis=1) * (dt * x)
            line = jnp.sum(jnp.concatenate([c_all[g]] * reps, axis=1) * new, axis=0, keepdims=True)
            h[g, :, c] = new
            y[pl.ds(g, 1), c] = line
        return 0

    lax.fori_loop(0, S, scan, 0)

    stay_slots = staying(out_slot, S, S - L)

    def scan_stay(i, _):
        g = stay_slots[0]
        for n in range(1, S - L):
            g = jnp.where(i == n, stay_slots[n], g)
        for c in chunks(C, 2048):
            reps = (c.stop - c.start) // HD
            dt = dt_two[pl.ds(g, 1), c]
            x = xc_two[pl.ds(g, 1), c]
            new = jnp.exp(-dt * rate[:, c]) * h[g, :, c]
            new += jnp.concatenate([b_two[g]] * reps, axis=1) * (dt * x)
            line = jnp.sum(jnp.concatenate([c_two[g]] * reps, axis=1) * new, axis=0, keepdims=True)
            stay[i, :, c] = new
            y_stay[pl.ds(i, 1), c] = line
        return 0

    lax.fori_loop(0, S - L, scan_stay, 0)
    save(stay, stay_out)
    save(y_stay, y_out)
    for c in chunks(C):
        m_buf[:, c] = (
            (y[:, c] + skip[:, c] * xc_all[:S, c]) * silu(mz[0, :, c].astype(F32))
        ).astype(BF16)

    save(m_buf, m_one)

    lax.fori_loop(1, R, lambda k, _: (att_copy(k).wait(), 0)[1], 0)
    for g in range(S):
        row, lane = source(g)
        tile = jnp.where(row >= S, got_att[lane].astype(F32), att_two[g].astype(F32))
        att_flat[1, g : g + 1] = line_up(tile)
    att_bf[...] = att_flat[...].astype(BF16)
    save(att_bf, att_out)
    for copy in saves:
        copy.wait()
    lax.fori_loop(1, R, lambda k, _: (state_copy(k).wait(), 0)[1], 0)


def finish_kernel(
    sizes,
    moves,
    stay,
    got_state,
    att_in,
    fconv_in,
    m_one,
    vec_moved_hbm,
    b_moved_hbm,
    vec_two_hbm,
    bc_two_hbm,
    y_hbm,
    a_log_hbm,
    skip_hbm,
    mz_hbm,
    att,
    out,
    final,
    fconv,
    arrived,
    done,
    vec_moved,
    b_moved,
    vec_two,
    bc_two,
    y_stay,
    rate,
    skip,
    mz,
    y,
    m_two,
    stay_v,
    att_v,
    fconv_v,
    m_v,
    first_sem,
    load_sem,
    arrive_sem,
    stay_sem,
    done_sem,
    pass_sem,
):
    R, S, L = sizes
    C = final.shape[2]
    me = lax.axis_index("replica")
    shift = [lax.div(moves[1, j], S) for j in range(L)]
    slot = [lax.rem(moves[1, lax.rem(me - shift[j] + R, R) * L + j], S) for j in range(L)]
    pairs = [
        (a_log_hbm, rate),
        (vec_moved_hbm, vec_moved),
        (b_moved_hbm, b_moved),
        (vec_two_hbm, vec_two),
        (bc_two_hbm, bc_two),
        (y_hbm, y_stay),
        (skip_hbm, skip),
        (mz_hbm, mz),
    ]
    loads = [
        pltpu.make_async_copy(src, dst, load_sem.at[i]) for i, (src, dst) in enumerate(pairs)
    ]
    arrivals = [
        pltpu.make_async_copy(
            got_state.at[jnp.maximum(shift[j] - 1, 0)], arrived.at[j], arrive_sem.at[j]
        )
        for j in range(L)
    ]
    for load in loads[:5]:
        load.start()
    for copy in arrivals:
        copy.start()
    for load in loads[5:]:
        load.start()
    firsts = [
        pltpu.make_async_copy(src, dst, first_sem.at[i])
        for i, (src, dst) in enumerate(
            [(stay, stay_v), (att_in, att_v), (fconv_in, fconv_v), (m_one, m_v)]
        )
    ]
    for copy in firsts:
        copy.start()
    stay_slots = staying(slot, S, S - L)
    passes = [
        pltpu.make_async_copy(stay_v.at[i], final.at[stay_slots[i]], stay_sem.at[i])
        for i in range(S - L)
    ] + [
        pltpu.make_async_copy(att_v, att, pass_sem.at[0]),
        pltpu.make_async_copy(fconv_v, fconv, pass_sem.at[1]),
        pltpu.make_async_copy(m_v, out.at[0], pass_sem.at[2]),
    ]
    wide = lambda v, c: jnp.concatenate([v] * ((c.stop - c.start) // HD), axis=1)
    for load in loads:
        load.wait()
    rate[...] = jnp.exp(rate[...])
    for copy in firsts:
        copy.wait()
    for copy in passes:
        copy.start()
    for i in range(S - L):
        y[pl.ds(stay_slots[i], 1), :] = y_stay[i : i + 1]
    results = []
    for j in range(L):
        g = slot[j]
        arrivals[j].wait()
        for c in chunks(C, 1024):
            dt, x = vec_moved[0, j : j + 1, c], vec_moved[1, j : j + 1, c]
            new = jnp.exp(-dt * rate[:, c]) * arrived[j, :, c].astype(F32)
            new += wide(b_moved[j], c) * (dt * x)
            dt, x = vec_two[0, pl.ds(g, 1), c], vec_two[1, pl.ds(g, 1), c]
            new = jnp.exp(-dt * rate[:, c]) * new + wide(bc_two[0, g], c) * (dt * x)
            line = jnp.sum(wide(bc_two[1, g], c) * new, axis=0, keepdims=True)
            done[j, :, c] = new
            y[pl.ds(g, 1), c] = line
        copy = pltpu.make_async_copy(done.at[j], final.at[g], done_sem.at[j])
        copy.start()
        results.append(copy)
    for c in chunks(C):
        m_two[:, c] = (
            (y[:, c] + skip[:, c] * vec_two[1, :, c]) * silu(mz[1, :, c].astype(F32))
        ).astype(BF16)
    last = pltpu.make_async_copy(m_two, out.at[1], pass_sem.at[3])
    last.start()
    for copy in passes + results + [last]:
        copy.wait()


def staying(moved, slots, count):
    found = [jnp.int32(0)] * count
    seen = jnp.int32(0)
    for g in range(slots):
        gone = moved[0] == g
        for slot in moved[1:]:
            gone = gone | (slot == g)
        for i in range(count):
            found[i] = jnp.where(~gone & (seen == i), g, found[i])
        seen = seen + jnp.where(gone, 0, 1)
    return found


def shards(
    lengths,
    page_table,
    key_pool,
    value_pool,
    queries,
    new_keys,
    new_values,
    conv_state,
    ssm_state,
    mamba_x,
    mamba_z,
    conv_weight,
    conv_bias,
    dt_down,
    bc_proj,
    dt_up,
    dt_bias,
    a_log,
    skip_d,
    moves,
):
    R, T = lax.axis_size("replica"), lax.axis_size("tensor")
    S, N, C = ssm_state.shape
    L = moves.shape[0] // R
    QW, W = queries.shape[2], key_pool.shape[2]
    H, KV = QW // HD, W // HD
    A = round_up(H + 2 * KV, 16)
    AH = round_up(H, 16)
    NR = S + round_up(L, 16)
    rank = dt_down.shape[1]

    row = lambda v: v.reshape(1, C)
    shape = jax.ShapeDtypeStruct
    dma = pltpu.SemaphoreType.DMA
    vm = lambda dims, kind=F32: pltpu.VMEM(dims, kind)
    like = lambda v: pltpu.VMEM(v.shape, v.dtype)
    NM = NR - S
    turned = moves.T
    operands = (
        jnp.transpose(conv_state, (1, 0, 2)),
        mamba_x,
        queries,
        new_keys,
        new_values,
        ssm_state,
        key_pool,
        value_pool,
        conv_weight,
        row(conv_bias),
        dt_down,
        bc_proj.T,
        dt_up,
        row(dt_bias),
        a_log,
        row(skip_d),
        mamba_z,
    )
    results = pl.pallas_call(
        functools.partial(exchange_kernel, (R, T, S, L, H, KV)),
        out_shape=(
            shape((S - L, N, C), F32),
            shape((R - 1, N, C), BF16),
            shape((2, S, QW), BF16),
            shape((3, S, C), F32),
            shape((S, C), BF16),
            shape((2, NM, C), F32),
            shape((NM, N, HD), F32),
            shape((2, S, C), F32),
            shape((2, S, N, HD), F32),
            shape((S - L, C), F32),
        ),
        in_specs=[SMEM] * 3 + [ANY] * len(operands),
        out_specs=(ANY,) * 10,
        scratch_shapes=[vm((4, NR, C))]
        + [like(v) for v in operands[1:]]
        + [
            vm((2, S, QW + 2 * W)),
            vm((2, S, A, HD), BF16),
            vm((L, 16, C // 4), BF16),
            vm((R - 1, N, C), BF16),
            vm((R - 1, 16, C // 4), BF16),
            vm((R - 1, 16, C // 4), BF16),
            vm((R - 1, A, HD), BF16),
            vm((R - 1, A, HD), BF16),
            vm((S, AH, HD), BF16),
            vm((R - 1, AH, HD), BF16),
            vm((R - 1, AH, HD), BF16),
            vm((4, S, C)),
            vm((NR, C)),
            vm((NR, C)),
            vm((NR, N, HD)),
            vm((NR, N, HD)),
            vm((S, C)),
            vm((S, C)),
            vm((S, N, HD)),
            vm((S, N, HD)),
            vm((N, C)),
            vm((S, C)),
            vm((S - L, C)),
            vm((S - L, N, C)),
            vm((2, S, QW)),
            vm((2, S, QW), BF16),
            vm((S, C), BF16),
            vm((T, NR, rank + HD)),
            vm((T, S, rank + HD)),
            dma((len(operands) + 2,)),
            dma((12,)),
        ]
        + [dma((R - 1,))] * 8
        + [dma((2, T))] * 2,
        compiler_params=pltpu.CompilerParams(
            collective_id=0, has_side_effects=True, vmem_limit_bytes=58 * 1024 * 1024
        ),
        name="exchange",
    )(turned, lengths, page_table.T, *operands)
    att, mamba_out, final_ssm, fconv = pl.pallas_call(
        functools.partial(finish_kernel, (R, S, L)),
        in_specs=[SMEM] + [ANY] * 13,
        out_specs=[ANY] * 4,
        out_shape=(
            shape((2, S, QW), BF16),
            shape((2, S, C), BF16),
            shape((S, N, C), F32),
            shape((3, S, C), F32),
        ),
        scratch_shapes=[
            vm((L, N, C), BF16),
            vm((L, N, C)),
            vm((2, NM, C)),
            vm((NM, N, HD)),
            vm((2, S, C)),
            vm((2, S, N, HD)),
            vm((S - L, C)),
            vm((N, C)),
            vm((1, C)),
            vm((2, S, C), BF16),
            vm((S, C)),
            vm((S, C), BF16),
            vm((S - L, N, C)),
            vm((2, S, QW), BF16),
            vm((3, S, C)),
            vm((S, C), BF16),
            dma((4,)),
            dma((8,)),
            dma((L,)),
            dma((S - L,)),
            dma((L,)),
            dma((4,)),
        ],
        compiler_params=pltpu.CompilerParams(vmem_limit_bytes=58 * 1024 * 1024),
        name="finish",
    )(turned, *results, a_log, row(skip_d), mamba_z)
    return att, mamba_out, final_ssm, jnp.transpose(fconv, (1, 0, 2))


def solution(mesh):
    row, both = P("replica", None, "tensor"), P(None, "replica", "tensor")
    in_specs = (
        P(),
        P("replica", None),
        row,
        row,
        both,
        both,
        both,
        row,
        row,
        both,
        both,
        P(None, "tensor"),
        P("tensor"),
        P("tensor", None),
        P("tensor", None),
        P(None, "tensor"),
        P("tensor"),
        P(None, "tensor"),
        P("tensor"),
        P(),
    )
    return jax.shard_map(
        shards, mesh=mesh, in_specs=in_specs, out_specs=(both, both, row, row), check_vma=False
    )
```

```python
import functools
import math

import jax
import jax.numpy as jnp
from jax import lax
from jax.experimental import pallas as pl
from jax.experimental.pallas import tpu as pltpu
from jax.sharding import PartitionSpec as P

HD = 128
F32, BF16 = jnp.float32, jnp.bfloat16
MESH = pl.DeviceIdType.MESH
ANY = pl.BlockSpec(memory_space=pl.ANY)
SMEM = pl.BlockSpec(memory_space=pltpu.SMEM)


def round_up(n, m):
    return (n + m - 1) // m * m


def silu(v):
    return v / (1.0 + jnp.exp(-v))


def softplus(v):
    return jnp.maximum(v, 0.0) + jnp.log1p(jnp.exp(-jnp.abs(v)))


def chunks(total, most=512):
    step = min(most, total)
    return [slice(i, i + step) for i in range(0, total, step)]


def exchange_kernel(
    sizes,
    moves,
    lengths,
    pages,
    conv_hbm,
    mx_hbm,
    q_hbm,
    nk_hbm,
    nv_hbm,
    states_hbm,
    keys_hbm,
    vals_hbm,
    conv_w_hbm,
    conv_b_hbm,
    down_hbm,
    bc_hbm,
    up_hbm,
    dt_b_hbm,
    a_log_hbm,
    skip_hbm,
    mz_hbm,
    stay_out,
    got_state,
    att_out,
    fconv,
    m_one,
    vec_moved,
    b_moved,
    vec_two,
    bc_two,
    y_out,
    win,
    mx,
    queries,
    nk,
    nv,
    h,
    keys,
    vals,
    conv_w,
    conv_b,
    down,
    bc_w,
    up,
    dt_b,
    a_log,
    skip,
    mz,
    flat,
    asks,
    pack,
    send_state,
    send_small,
    got_small,
    send_ask,
    got_ask,
    att_two,
    send_att,
    got_att,
    win_two,
    xc_all,
    dt_all,
    b_all,
    c_all,
    xc_two,
    dt_two,
    b_two,
    c_two,
    rate,
    y,
    y_stay,
    stay,
    att_flat,
    att_bf,
    m_buf,
    part,
    part_two,
    load_sem,
    save_sem,
    state_s,
    state_r,
    small_s,
    small_r,
    ask_s,
    ask_r,
    att_s,
    att_r,
    part_s,
    part_r,
):
    R, T, S, L, H, KV = sizes
    C = h.shape[2]
    N = a_log.shape[0]
    NR = win.shape[1]
    rank = down.shape[1]
    page = keys.shape[1]
    n_pages = pages.shape[0]
    QW, W = queries.shape[2], keys.shape[2]
    A = asks.shape[2]
    me = lax.axis_index("replica")
    core = lax.axis_index("tensor")

    pairs = [(conv_hbm.at[k], win.at[k, pl.ds(0, S)]) for k in range(3)] + [
        (mx_hbm, mx),
        (q_hbm, queries),
        (nk_hbm, nk),
        (nv_hbm, nv),
        (states_hbm, h),
        (keys_hbm, keys),
        (vals_hbm, vals),
        (conv_w_hbm, conv_w),
        (conv_b_hbm, conv_b),
        (down_hbm, down),
        (bc_hbm, bc_w),
        (up_hbm, up),
        (dt_b_hbm, dt_b),
        (a_log_hbm, a_log),
        (skip_hbm, skip),
        (mz_hbm, mz),
    ]
    loads = [
        pltpu.make_async_copy(src, dst, load_sem.at[i]) for i, (src, dst) in enumerate(pairs)
    ]
    loads[7].start()
    for load in loads[:7] + loads[8:]:
        load.start()
    saves = []

    def save(src, dst):
        copy = pltpu.make_async_copy(src, dst, save_sem.at[len(saves)])
        copy.start()
        saves.append(copy)

    barrier = pltpu.get_barrier_semaphore()

    def greet(k, _):
        pl.semaphore_signal(
            barrier, inc=1, device_id={"replica": lax.rem(me + k, R)}, device_id_type=MESH
        )
        return 0

    def greet_core(k, _):
        pl.semaphore_signal(
            barrier, inc=1, device_id={"tensor": lax.rem(core + k, T)}, device_id_type=MESH
        )
        return 0

    lax.fori_loop(1, R, greet, 0)
    lax.fori_loop(1, T, greet_core, 0)

    shift = [lax.div(moves[1, j], S) for j in range(L)]
    out_slot = [lax.rem(moves[0, me * L + j], S) for j in range(L)]
    lane_of = [jnp.maximum(shift[j] - 1, 0) for j in range(L)]
    in_slot = [
        lax.rem(moves[1, lax.rem(me - shift[j] + R, R) * L + j], S) for j in range(L)
    ]

    def pick(values, k):
        found = values[0]
        for j in range(1, L):
            found = jnp.where(shift[j] == k, values[j], found)
        return found

    def source(g):
        row, lane = g, 0
        for j in range(L):
            hit = in_slot[j] == g
            row = jnp.where(hit, S + j, row)
            lane = jnp.where(hit, lane_of[j], lane)
        return row, lane

    def lane_copy(src, dst, send, recv, k, forward=True):
        to = lax.rem(me + k, R) if forward else lax.rem(me - k + R, R)
        return pltpu.make_async_remote_copy(
            src_ref=src.at[k - 1],
            dst_ref=dst.at[k - 1],
            send_sem=send.at[k - 1],
            recv_sem=recv.at[k - 1],
            device_id={"replica": to},
            device_id_type=MESH,
        )

    ask_copy = lambda k: lane_copy(send_ask, got_ask, ask_s, ask_r, k, False)
    small_copy = lambda k: lane_copy(send_small, got_small, small_s, small_r, k)
    state_copy = lambda k: lane_copy(send_state, got_state, state_s, state_r, k)
    att_copy = lambda k: lane_copy(send_att, got_att, att_s, att_r, k)

    pl.semaphore_wait(barrier, R - 1 + T - 1)

    def lane(i):
        return 1 + lax.rem(7 * i + 4 * me, R - 1)

    def send_states(i, _):
        k = lane(i)
        slot = pick(out_slot, k)
        for c in chunks(C):
            send_state[k - 1, :, c] = h[slot, :, c].astype(BF16)
        state_copy(k).start()
        return 0

    def send_small_rows(i, _):
        k = lane(i)
        send_small[k - 1] = pack[pick(range(L), k)]
        small_copy(k).start()
        return 0

    def send_asks(i, _):
        k = lane(i)
        send_ask[k - 1] = asks[1, pick(in_slot, k)]
        ask_copy(k).start()
        return 0

    early = min(4, R - 1)
    loads[7].wait()
    lax.fori_loop(0, early, send_states, 0)

    for load in loads[4:7]:
        load.wait()
    for t in range(2):
        flat[t, :, :QW] = queries[t].astype(F32)
        flat[t, :, QW : QW + W] = nk[t].astype(F32)
        flat[t, :, QW + W :] = nv[t].astype(F32)

    def tile_up(g, _):
        for t in range(2):
            line = flat[t, pl.ds(g, 1), :]
            parts = [line[:, i * HD : (i + 1) * HD] for i in range(H + 2 * KV)]
            if A > H + 2 * KV:
                parts.append(jnp.zeros((A - H - 2 * KV, HD), F32))
            asks[t, g] = jnp.concatenate(parts, axis=0).astype(BF16)
        return 0

    lax.fori_loop(0, S, tile_up, 0)

    for load in loads[:4]:
        load.wait()
    win[3, :S] = mx[0].astype(F32)
    for j in range(L):
        lines = [win[k, pl.ds(out_slot[j], 1), :] for k in range(4)]
        pack[j] = jnp.concatenate(
            [line[:, i * (C // 4) : (i + 1) * (C // 4)] for line in lines for i in range(4)],
            axis=0,
        ).astype(BF16)

    lax.fori_loop(0, R - 1, send_asks, 0)
    lax.fori_loop(0, R - 1, send_small_rows, 0)
    lax.fori_loop(early, R - 1, send_states, 0)

    loads[8].wait()
    loads[9].wait()
    lax.fori_loop(1, R, lambda k, _: (ask_copy(k).wait(), 0)[1], 0)

    rows = 2 * H
    head_of = lax.broadcasted_iota(jnp.int32, (rows, 1), 0) % H // (H // KV)
    step_of = lax.broadcasted_iota(jnp.int32, (rows, 1), 0) // H
    ask_col = lax.broadcasted_iota(jnp.int32, (rows, asks.shape[2]), 1)
    pos = lax.broadcasted_iota(jnp.int32, (rows, n_pages * page), 1)
    is_key = ask_col == H + head_of
    is_val = ask_col == H + KV + head_of
    nt = (((1,), (1,)), ((), ()))
    nn = (((1,), (0,)), ((), ()))

    def line_up(tile):
        return jnp.concatenate([tile[i : i + 1] for i in range(H)], axis=1)

    def attend(g):
        length = lengths[me * S + g]
        gone = jnp.int32(0)
        lane = jnp.int32(0)
        for j in range(L):
            hit = out_slot[j] == g
            gone = jnp.where(hit, 1, gone)
            lane = jnp.where(hit, lane_of[j], lane)
        one = asks[0, g]
        two = jnp.where(gone == 1, got_ask[lane].astype(F32), asks[1, g].astype(F32)).astype(BF16)
        q = jnp.concatenate([one.astype(F32)[:H], two.astype(F32)[:H]], axis=0)
        qb = q.astype(BF16)
        wide = jnp.concatenate(
            [jnp.where(head_of == i, q, 0.0) for i in range(KV)], axis=1
        ).astype(BF16)
        scores = jnp.concatenate(
            [
                lax.dot_general(wide, keys[pages[p, g]], nt, preferred_element_type=F32)
                for p in range(n_pages)
            ],
            axis=1,
        )
        new_one = lax.dot_general(qb, one, nt, preferred_element_type=F32)
        new_two = lax.dot_general(qb, two, nt, preferred_element_type=F32)
        new_one = jnp.sum(jnp.where(is_key, new_one, 0.0), axis=1, keepdims=True)
        new_two = jnp.sum(jnp.where(is_key, new_two, 0.0), axis=1, keepdims=True)
        at_one, at_two = pos == length, pos == length + 1
        scores = jnp.where(at_one, new_one, jnp.where(at_two, new_two, scores))
        scores = scores * (1.0 / math.sqrt(HD))
        scores = jnp.where(pos <= length + step_of, scores, -1e30)
        expo = jnp.exp(scores - jnp.max(scores, axis=1, keepdims=True))
        w = expo / jnp.sum(expo, axis=1, keepdims=True)
        w_one = jnp.sum(jnp.where(at_one, w, 0.0), axis=1, keepdims=True)
        w_two = jnp.sum(jnp.where(at_two, w, 0.0), axis=1, keepdims=True)
        w = jnp.where(at_one | at_two, 0.0, w).astype(BF16)
        mixed = lax.dot_general(
            w[:, :page], vals[pages[0, g]], nn, preferred_element_type=F32
        )
        for p in range(1, n_pages):
            mixed += lax.dot_general(
                w[:, p * page : (p + 1) * page],
                vals[pages[p, g]],
                nn,
                preferred_element_type=F32,
            )
        out = lax.dot_general(
            jnp.where(is_val, w_one, 0.0).astype(BF16), one, nn, preferred_element_type=F32
        ) + lax.dot_general(
            jnp.where(is_val, w_two, 0.0).astype(BF16), two, nn, preferred_element_type=F32
        )
        for i in range(KV):
            out += jnp.where(head_of == i, mixed[:, i * HD : (i + 1) * HD], 0.0)
        first, second = out[:H], out[H:]
        if att_two.shape[1] > H:
            pad = jnp.zeros((att_two.shape[1] - H, HD), F32)
            first = jnp.concatenate([first, pad], axis=0)
            second = jnp.concatenate([second, pad], axis=0)
        return first.astype(BF16), second.astype(BF16)

    batch = 4 if S % 4 == 0 else 1

    def attend_some(i, _):
        results = [attend(i * batch + b) for b in range(batch)]
        for b, (first, second) in enumerate(results):
            att_flat[0, pl.ds(i * batch + b, 1), :] = line_up(first.astype(F32))
            att_two[i * batch + b] = second
        return 0

    lax.fori_loop(0, S // batch, attend_some, 0)

    def send_back(k, _):
        send_att[k - 1] = att_two[pick(out_slot, k)]
        att_copy(k).start()
        return 0

    lax.fori_loop(1, R, send_back, 0)

    lax.fori_loop(1, R, lambda k, _: (small_copy(k).wait(), 0)[1], 0)
    for j in range(L):
        tile = got_small[lane_of[j]].astype(F32)
        for k in range(4):
            win[k, S + j : S + j + 1] = jnp.concatenate(
                [tile[4 * k + i : 4 * k + i + 1] for i in range(4)], axis=1
            )
    for k in range(4):
        win[k, S + L :] = jnp.zeros((NR - S - L, C), F32)

    def project(src, n, xc_ref, buf):
        low = jnp.zeros((n, rank), F32)
        bc = jnp.zeros((n, bc_w.shape[0]), F32)
        for c in chunks(C):
            total = conv_b[:, c] + src(0, c) * conv_w[0:1, c]
            for k in range(1, 4):
                total += src(k, c) * conv_w[k : k + 1, c]
            xb = silu(total).astype(BF16)
            xc_ref[:, c] = xb.astype(F32)
            low += lax.dot_general(xb, down[c], nn, preferred_element_type=F32)
            bc += lax.dot_general(xb, bc_w[:, c], nt, preferred_element_type=F32)
        buf[core, :, :rank] = low
        buf[core, :, rank:] = jnp.concatenate(
            [bc, jnp.zeros((n, HD - bc.shape[1]), F32)], axis=1
        )

    def core_copy(buf, which, k):
        return pltpu.make_async_remote_copy(
            src_ref=buf.at[core],
            dst_ref=buf.at[core],
            send_sem=part_s.at[which, k],
            recv_sem=part_r.at[which, k],
            device_id={"tensor": lax.rem(core + k, T)},
            device_id_type=MESH,
        )

    def reduce_parts(buf, which):
        lax.fori_loop(1, T, lambda k, _: (core_copy(buf, which, k).start(), 0)[1], 0)
        lax.fori_loop(1, T, lambda k, _: (core_copy(buf, which, k).wait(), 0)[1], 0)
        total = buf[0]
        for t in range(1, T):
            total += buf[t]
        return total

    def steps(total, n, dt_ref, b_ref, c_ref):
        low = total[:, :rank].astype(BF16)
        for c in chunks(C):
            dt_ref[:, c] = softplus(
                lax.dot_general(low, up[:, c], nn, preferred_element_type=F32) + dt_b[:, c]
            )
        turned = total[:, rank : rank + HD].T
        for i in range(n):
            b_ref[i] = jnp.broadcast_to(turned[:N, i : i + 1], (N, HD))
            c_ref[i] = jnp.broadcast_to(turned[N : 2 * N, i : i + 1], (N, HD))

    for load in loads[10:]:
        load.wait()
    rate[...] = jnp.exp(a_log[...])
    project(lambda k, c: win[k, :, c], NR, xc_all, part)
    steps(reduce_parts(part, 0), NR, dt_all, b_all, c_all)
    moved = pl.ds(S, NR - S)
    save(dt_all.at[moved], vec_moved.at[0])
    save(xc_all.at[moved], vec_moved.at[1])
    save(b_all.at[moved], b_moved)

    for g in range(S):
        row, _ = source(g)
        for k in range(3):
            win_two[k, g : g + 1] = win[k + 1, pl.ds(row, 1), :]
    win_two[3] = mx[1].astype(F32)
    save(win_two.at[pl.ds(1, 3)], fconv)
    project(lambda k, c: win_two[k, :, c], S, xc_two, part_two)
    steps(reduce_parts(part_two, 1), S, dt_two, b_two, c_two)
    save(dt_two, vec_two.at[0])
    save(xc_two, vec_two.at[1])
    save(b_two, bc_two.at[0])
    save(c_two, bc_two.at[1])

    def scan(g, _):
        for c in chunks(C, 2048):
            reps = (c.stop - c.start) // HD
            dt = dt_all[pl.ds(g, 1), c]
            x = xc_all[pl.ds(g, 1), c]
            new = jnp.exp(-dt * rate[:, c]) * h[g, :, c]
            new += jnp.concatenate([b_all[g]] * reps, axis=1) * (dt * x)
            line = jnp.sum(jnp.concatenate([c_all[g]] * reps, axis=1) * new, axis=0, keepdims=True)
            h[g, :, c] = new
            y[pl.ds(g, 1), c] = line
        return 0

    lax.fori_loop(0, S, scan, 0)

    stay_slots = staying(out_slot, S, S - L)

    def scan_stay(i, _):
        g = stay_slots[0]
        for n in range(1, S - L):
            g = jnp.where(i == n, stay_slots[n], g)
        for c in chunks(C, 2048):
            reps = (c.stop - c.start) // HD
            dt = dt_two[pl.ds(g, 1), c]
            x = xc_two[pl.ds(g, 1), c]
            new = jnp.exp(-dt * rate[:, c]) * h[g, :, c]
            new += jnp.concatenate([b_two[g]] * reps, axis=1) * (dt * x)
            line = jnp.sum(jnp.concatenate([c_two[g]] * reps, axis=1) * new, axis=0, keepdims=True)
            stay[i, :, c] = new
            y_stay[pl.ds(i, 1), c] = line
        return 0

    lax.fori_loop(0, S - L, scan_stay, 0)
    save(stay, stay_out)
    save(y_stay, y_out)
    for c in chunks(C):
        m_buf[:, c] = (
            (y[:, c] + skip[:, c] * xc_all[:S, c]) * silu(mz[0, :, c].astype(F32))
        ).astype(BF16)

    save(m_buf, m_one)

    lax.fori_loop(1, R, lambda k, _: (att_copy(k).wait(), 0)[1], 0)
    for g in range(S):
        row, lane = source(g)
        tile = jnp.where(row >= S, got_att[lane].astype(F32), att_two[g].astype(F32))
        att_flat[1, g : g + 1] = line_up(tile)
    att_bf[...] = att_flat[...].astype(BF16)
    save(att_bf, att_out)
    for copy in saves:
        copy.wait()
    lax.fori_loop(1, R, lambda k, _: (state_copy(k).wait(), 0)[1], 0)


def finish_kernel(
    sizes,
    moves,
    stay,
    got_state,
    att_in,
    fconv_in,
    m_one,
    vec_moved_hbm,
    b_moved_hbm,
    vec_two_hbm,
    bc_two_hbm,
    y_hbm,
    a_log_hbm,
    skip_hbm,
    mz_hbm,
    att,
    out,
    final,
    fconv,
    arrived,
    done,
    vec_moved,
    b_moved,
    vec_two,
    bc_two,
    y_stay,
    rate,
    skip,
    mz,
    y,
    m_two,
    stay_v,
    att_v,
    fconv_v,
    m_v,
    first_sem,
    load_sem,
    arrive_sem,
    stay_sem,
    done_sem,
    pass_sem,
):
    R, S, L = sizes
    C = final.shape[2]
    me = lax.axis_index("replica")
    shift = [lax.div(moves[1, j], S) for j in range(L)]
    slot = [lax.rem(moves[1, lax.rem(me - shift[j] + R, R) * L + j], S) for j in range(L)]
    pairs = [
        (a_log_hbm, rate),
        (vec_moved_hbm, vec_moved),
        (b_moved_hbm, b_moved),
        (vec_two_hbm, vec_two),
        (bc_two_hbm, bc_two),
        (y_hbm, y_stay),
        (skip_hbm, skip),
        (mz_hbm, mz),
    ]
    loads = [
        pltpu.make_async_copy(src, dst, load_sem.at[i]) for i, (src, dst) in enumerate(pairs)
    ]
    arrivals = [
        pltpu.make_async_copy(
            got_state.at[jnp.maximum(shift[j] - 1, 0)], arrived.at[j], arrive_sem.at[j]
        )
        for j in range(L)
    ]
    for load in loads[:5]:
        load.start()
    for copy in arrivals:
        copy.start()
    for load in loads[5:]:
        load.start()
    firsts = [
        pltpu.make_async_copy(src, dst, first_sem.at[i])
        for i, (src, dst) in enumerate(
            [(stay, stay_v), (att_in, att_v), (fconv_in, fconv_v), (m_one, m_v)]
        )
    ]
    for copy in firsts:
        copy.start()
    stay_slots = staying(slot, S, S - L)
    passes = [
        pltpu.make_async_copy(stay_v.at[i], final.at[stay_slots[i]], stay_sem.at[i])
        for i in range(S - L)
    ] + [
        pltpu.make_async_copy(att_v, att, pass_sem.at[0]),
        pltpu.make_async_copy(fconv_v, fconv, pass_sem.at[1]),
        pltpu.make_async_copy(m_v, out.at[0], pass_sem.at[2]),
    ]
    wide = lambda v, c: jnp.concatenate([v] * ((c.stop - c.start) // HD), axis=1)
    for load in loads:
        load.wait()
    rate[...] = jnp.exp(rate[...])
    for copy in firsts:
        copy.wait()
    for copy in passes:
        copy.start()
    for i in range(S - L):
        y[pl.ds(stay_slots[i], 1), :] = y_stay[i : i + 1]
    results = []
    for j in range(L):
        g = slot[j]
        arrivals[j].wait()
        for c in chunks(C, 1024):
            dt, x = vec_moved[0, j : j + 1, c], vec_moved[1, j : j + 1, c]
            new = jnp.exp(-dt * rate[:, c]) * arrived[j, :, c].astype(F32)
            new += wide(b_moved[j], c) * (dt * x)
            dt, x = vec_two[0, pl.ds(g, 1), c], vec_two[1, pl.ds(g, 1), c]
            new = jnp.exp(-dt * rate[:, c]) * new + wide(bc_two[0, g], c) * (dt * x)
            line = jnp.sum(wide(bc_two[1, g], c) * new, axis=0, keepdims=True)
            done[j, :, c] = new
            y[pl.ds(g, 1), c] = line
        copy = pltpu.make_async_copy(done.at[j], final.at[g], done_sem.at[j])
        copy.start()
        results.append(copy)
    for c in chunks(C):
        m_two[:, c] = (
            (y[:, c] + skip[:, c] * vec_two[1, :, c]) * silu(mz[1, :, c].astype(F32))
        ).astype(BF16)
    last = pltpu.make_async_copy(m_two, out.at[1], pass_sem.at[3])
    last.start()
    for copy in passes + results + [last]:
        copy.wait()


def staying(moved, slots, count):
    found = [jnp.int32(0)] * count
    seen = jnp.int32(0)
    for g in range(slots):
        gone = moved[0] == g
        for slot in moved[1:]:
            gone = gone | (slot == g)
        for i in range(count):
            found[i] = jnp.where(~gone & (seen == i), g, found[i])
        seen = seen + jnp.where(gone, 0, 1)
    return found


def shards(
    lengths,
    page_table,
    key_pool,
    value_pool,
    queries,
    new_keys,
    new_values,
    conv_state,
    ssm_state,
    mamba_x,
    mamba_z,
    conv_weight,
    conv_bias,
    dt_down,
    bc_proj,
    dt_up,
    dt_bias,
    a_log,
    skip_d,
    moves,
):
    R, T = lax.axis_size("replica"), lax.axis_size("tensor")
    S, N, C = ssm_state.shape
    L = moves.shape[0] // R
    QW, W = queries.shape[2], key_pool.shape[2]
    H, KV = QW // HD, W // HD
    A = round_up(H + 2 * KV, 16)
    AH = round_up(H, 16)
    NR = S + round_up(L, 16)
    rank = dt_down.shape[1]

    row = lambda v: v.reshape(1, C)
    shape = jax.ShapeDtypeStruct
    dma = pltpu.SemaphoreType.DMA
    vm = lambda dims, kind=F32: pltpu.VMEM(dims, kind)
    like = lambda v: pltpu.VMEM(v.shape, v.dtype)
    NM = NR - S
    turned = moves.T
    operands = (
        jnp.transpose(conv_state, (1, 0, 2)),
        mamba_x,
        queries,
        new_keys,
        new_values,
        ssm_state,
        key_pool,
        value_pool,
        conv_weight,
        row(conv_bias),
        dt_down,
        bc_proj.T,
        dt_up,
        row(dt_bias),
        a_log,
        row(skip_d),
        mamba_z,
    )
    results = pl.pallas_call(
        functools.partial(exchange_kernel, (R, T, S, L, H, KV)),
        out_shape=(
            shape((S - L, N, C), F32),
            shape((R - 1, N, C), BF16),
            shape((2, S, QW), BF16),
            shape((3, S, C), F32),
            shape((S, C), BF16),
            shape((2, NM, C), F32),
            shape((NM, N, HD), F32),
            shape((2, S, C), F32),
            shape((2, S, N, HD), F32),
            shape((S - L, C), F32),
        ),
        in_specs=[SMEM] * 3 + [ANY] * len(operands),
        out_specs=(ANY,) * 10,
        scratch_shapes=[vm((4, NR, C))]
        + [like(v) for v in operands[1:]]
        + [
            vm((2, S, QW + 2 * W)),
            vm((2, S, A, HD), BF16),
            vm((L, 16, C // 4), BF16),
            vm((R - 1, N, C), BF16),
            vm((R - 1, 16, C // 4), BF16),
            vm((R - 1, 16, C // 4), BF16),
            vm((R - 1, A, HD), BF16),
            vm((R - 1, A, HD), BF16),
            vm((S, AH, HD), BF16),
            vm((R - 1, AH, HD), BF16),
            vm((R - 1, AH, HD), BF16),
            vm((4, S, C)),
            vm((NR, C)),
            vm((NR, C)),
            vm((NR, N, HD)),
            vm((NR, N, HD)),
            vm((S, C)),
            vm((S, C)),
            vm((S, N, HD)),
            vm((S, N, HD)),
            vm((N, C)),
            vm((S, C)),
            vm((S - L, C)),
            vm((S - L, N, C)),
            vm((2, S, QW)),
            vm((2, S, QW), BF16),
            vm((S, C), BF16),
            vm((T, NR, rank + HD)),
            vm((T, S, rank + HD)),
            dma((len(operands) + 2,)),
            dma((12,)),
        ]
        + [dma((R - 1,))] * 8
        + [dma((2, T))] * 2,
        compiler_params=pltpu.CompilerParams(
            collective_id=0, has_side_effects=True, vmem_limit_bytes=58 * 1024 * 1024
        ),
        name="exchange",
    )(turned, lengths, page_table.T, *operands)
    att, mamba_out, final_ssm, fconv = pl.pallas_call(
        functools.partial(finish_kernel, (R, S, L)),
        in_specs=[SMEM] + [ANY] * 13,
        out_specs=[ANY] * 4,
        out_shape=(
            shape((2, S, QW), BF16),
            shape((2, S, C), BF16),
            shape((S, N, C), F32),
            shape((3, S, C), F32),
        ),
        scratch_shapes=[
            vm((L, N, C), BF16),
            vm((L, N, C)),
            vm((2, NM, C)),
            vm((NM, N, HD)),
            vm((2, S, C)),
            vm((2, S, N, HD)),
            vm((S - L, C)),
            vm((N, C)),
            vm((1, C)),
            vm((2, S, C), BF16),
            vm((S, C)),
            vm((S, C), BF16),
            vm((S - L, N, C)),
            vm((2, S, QW), BF16),
            vm((3, S, C)),
            vm((S, C), BF16),
            dma((4,)),
            dma((8,)),
            dma((L,)),
            dma((S - L,)),
            dma((L,)),
            dma((4,)),
        ],
        compiler_params=pltpu.CompilerParams(vmem_limit_bytes=58 * 1024 * 1024),
        name="finish",
    )(turned, *results, a_log, row(skip_d), mamba_z)
    return att, mamba_out, final_ssm, jnp.transpose(fconv, (1, 0, 2))


def solution(mesh):
    row, both = P("replica", None, "tensor"), P(None, "replica", "tensor")
    in_specs = (
        P(),
        P("replica", None),
        row,
        row,
        both,
        both,
        both,
        row,
        row,
        both,
        both,
        P(None, "tensor"),
        P("tensor"),
        P("tensor", None),
        P("tensor", None),
        P(None, "tensor"),
        P("tensor"),
        P(None, "tensor"),
        P("tensor"),
        P(),
    )
    return jax.shard_map(
        shards, mesh=mesh, in_specs=in_specs, out_specs=(both, both, row, row), check_vma=False
    )
```
